32 devices in a mesh: study: 16 (over z, y, x), cell: 2 (over core).
Axes of the slice: x: 2, y: 2, z: 4, core: 2. Of those that a mesh axis runs over, the one named last changes fastest.
Arguments:
- latents: bfloat16 [16, 1024, 64], P('study', 'cell'), may hold values from -8 to 8
- donor_ids: int32 [16, 1024], P('study', 'cell'), may hold values from 0 to 15, as said below
- study_valid_length: int32 [16], P('study'), may hold values from 1 to 1024, 12288 in all
- study_penalty_weight: float32 [16], P('study'), may hold values from 1 to 8
- frequencies: bfloat16 [64, 8192], replicated, may hold values from -0.75 to 0.75
- phases: float32 [8192], replicated, may hold values from -3.140625 to 3.140625
Outputs:
- latent_grad: float32 [16, 1024, 64], P('study', 'cell')
The draws below stay inside these ranges and needn't reach their ends.
Inputs may be any that keep to these rules, and one draw needn't show every extreme that they name: `donor_ids`: donor ids never fall along a study's window; every study's window begins with donor 0 and ends with donor 16 - 1.
All inputs are finite; a program needn't handle non-finite values. No bound on the sum of `study_valid_length` on one device may be relied on, other than what follows from the above.
Results may differ from the reference program's by a relative error of at most 0.00045.
Values may be sent and summed in bfloat16 or wider, within the bound.
No kernel may reach another device: no remote copies, remote signals or barrier semaphores. Data moves between devices by JAX's collectives and lax.ppermute only.
A program may use at most 64 MiB of HBM per device.

```python
import math
import jax
import jax.numpy as jnp
import numpy as np
from jax import lax

LATENT_SIZE = 64
FREQS = 8192
DONOR_LABELS = 16
CELL_DEV = 512
WINDOW_CELLS = 1024
STUDY_TOTAL = 16
N_CELL = 2


def donor_layout(key):
    window_edges = jnp.sort(jax.random.randint(jax.random.fold_in(key, 11), (STUDY_TOTAL, DONOR_LABELS - 1), 1, WINDOW_CELLS), axis=1)
    position = jnp.arange(WINDOW_CELLS, dtype=jnp.int32)
    return jnp.sum((position[None, :, None] >= window_edges[:, None, :]).astype(jnp.int32), axis=2)


def pick_rows(table, index):
    return table[index]


def draw_donor_ids(key, part):
    return donor_layout(key)


def draw_latents(key, part):
    donor_rows = donor_layout(key)
    study_random_key, donor_random_key, noise_random_key = jax.random.split(jax.random.fold_in(key, 23), 3)
    study_scale_draw = 0.3 * (1.0 + 2.0 * jnp.arange(STUDY_TOTAL, dtype=jnp.float32) / max(STUDY_TOTAL - 1, 1))
    study_offset_draw = jax.random.normal(study_random_key, (STUDY_TOTAL, LATENT_SIZE), jnp.float32) * study_scale_draw[:, None]
    donor_offset_draw = 0.5 * jax.random.normal(donor_random_key, (STUDY_TOTAL, DONOR_LABELS, LATENT_SIZE), jnp.float32)
    cell_shift = jax.vmap(pick_rows)(donor_offset_draw, donor_rows)
    noise_component = jax.random.normal(noise_random_key, (STUDY_TOTAL, WINDOW_CELLS, LATENT_SIZE), jnp.float32)
    return jnp.clip(noise_component + study_offset_draw[:, None, :] + cell_shift, -8.0, 8.0).astype(jnp.bfloat16)


def block_levels(rng, dims, cuts, low, top_value):
    def one(dim, parts):
        steps = jax.random.uniform(jax.random.fold_in(jax.random.fold_in(rng, 6), dim), (parts,), jnp.float32, low / len(cuts), top_value / len(cuts))
        return jnp.repeat(jnp.exp(steps), dims[dim] // parts).reshape((-1,) + (1,) * (len(dims) - dim - 1))

    gain = one(*cuts[0])
    for cut in cuts[1:]:
        gain = gain * one(*cut)
    return gain


def split_up(count, total, limit, skew):
    portions = [(1 << 20) // math.isqrt(rank ** skew) + 1 for rank in range(2, count + 1)]
    surplus, given = total - limit - (count - 1), [1] * (count - 1)
    while surplus > 0:
        candidates = [i for i in range(count - 1) if given[i] < limit]
        pool, budget = sum([portions[i] for i in candidates]), surplus
        for i in candidates:
            extra = min(limit - given[i], max(1, budget * portions[i] // pool), surplus)
            given[i] = given[i] + extra
            surplus = surplus - extra
    return np.array([limit] + given)


def ragged_sizes(key, count, total, most, lean):
    if count == 2:
        one = jax.random.randint(key, (), max(1, total - most), min(most, total - 1) + 1)
        return jnp.stack([one, total - one])
    sizes = jnp.asarray(split_up(count, total, most, lean), jnp.int32)
    pairs = (count - 1) // 2
    donor, taker = sizes[1:1 + 2 * pairs:2], sizes[2:2 + 2 * pairs:2]
    room = jnp.minimum(donor - 1, most - taker)
    passed = jax.random.randint(jax.random.fold_in(key, 1), (pairs,), 0, 1 << 20) % (room + 1)
    sizes = sizes.at[1:1 + 2 * pairs:2].set(donor - passed).at[2:2 + 2 * pairs:2].set(taker + passed)
    return sizes[jax.random.permutation(jax.random.fold_in(key, 2), count)]


def normal_values(stream_key, extent, deviation, limit, held_as=jnp.bfloat16):
    return jnp.clip(deviation * jax.random.normal(stream_key, extent, jnp.float32), -limit, limit).astype(held_as)


def setup_inputs(seed: int = 0) -> dict:
    arg_keys = jax.random.split(jax.random.key(seed), 7)
    latents = draw_latents(jax.random.fold_in(arg_keys[6], 71), 0)
    donor_ids = draw_donor_ids(jax.random.fold_in(arg_keys[6], 71), 0)
    study_valid_length = ragged_sizes(arg_keys[2], STUDY_TOTAL, STUDY_TOTAL * WINDOW_CELLS * 3 // 4, WINDOW_CELLS, 0).astype(jnp.int32)
    study_penalty_weight = jnp.clip(jnp.exp(math.log(8.0) - 2.0794415 * jax.random.uniform(arg_keys[3], (STUDY_TOTAL,), jnp.float32) ** block_levels(arg_keys[3], (STUDY_TOTAL,), ((0, 16),), -0.2, 0.2)), 1.0, 8.0)
    frequencies = normal_values(arg_keys[4], (LATENT_SIZE, FREQS), LATENT_SIZE ** -0.5, 0.75)
    phases = jnp.clip(jax.random.uniform(arg_keys[5], (FREQS,), jnp.float32, -3.140625, 3.140625), -3.140625, 3.140625)
    return dict(latents=latents, donor_ids=donor_ids, study_valid_length=study_valid_length, study_penalty_weight=study_penalty_weight, frequencies=frequencies, phases=phases)


feature_penalty = 16.0

def donor_counts(donor_row, validity):
    donors = jnp.arange(DONOR_LABELS, dtype=jnp.int32)
    member = (donor_row[None, :] == donors[:, None]).astype(jnp.float32)
    return (member, lax.optimization_barrier(jnp.sum(member * validity[None, :], axis=1)))

def coupling_tile(left_rows, left_donors, left_inverse, left_valid, right_rows, right_donors, right_inverse, right_valid, weight, inverse_n, present):
    left_sq = lax.optimization_barrier(jnp.sum(jnp.square(left_rows.astype(jnp.float32)), axis=1))
    right_sq = lax.optimization_barrier(jnp.sum(jnp.square(right_rows.astype(jnp.float32)), axis=1))
    inner = jnp.dot(left_rows, right_rows.T, preferred_element_type=jnp.float32)
    squared = left_sq[:, None] + right_sq[None, :] - 2.0 * inner
    kernel = jnp.exp(squared * (-0.5 / left_rows.shape[1]))
    same_donor = left_donors[:, None] == right_donors[None, :]
    pair_weight = jnp.where(same_donor, jnp.square(left_inverse)[:, None], 0.0) - inverse_n * (left_inverse[:, None] + right_inverse[None, :]) + present * inverse_n * inverse_n
    pair_mask = left_valid[:, None] * right_valid[None, :]
    return weight * pair_mask * pair_weight * kernel

def level_one(study_rows, study_donors, length, weight):
    position = jnp.arange(WINDOW_CELLS, dtype=jnp.int32)
    validity = (position < length).astype(jnp.float32)
    member, counts = donor_counts(study_donors, validity)
    inverse = 1.0 / jnp.maximum(counts, 1.0)
    present = jnp.sum((counts > 0.5).astype(jnp.float32))
    cell_inverse = lax.optimization_barrier(jnp.sum(member * inverse[:, None], axis=0))
    inverse_n = 1.0 / length.astype(jnp.float32)
    rows_wide = study_rows.astype(jnp.float32)

    def row_block(pieces):
        left_rows, left_donors, left_inverse, left_valid = pieces
        coupling = coupling_tile(left_rows, left_donors, left_inverse, left_valid, study_rows, study_donors, cell_inverse, validity, weight, inverse_n, present)
        row_sums = lax.optimization_barrier(jnp.sum(coupling, axis=1))
        weighted = jnp.dot(coupling, rows_wide, precision=lax.Precision.HIGHEST)
        return -(2.0 * WINDOW_CELLS / LATENT_SIZE) * (left_rows.astype(jnp.float32) * row_sums[:, None] - weighted)
    blocks = lax.map(row_block, (study_rows.reshape(N_CELL, CELL_DEV, LATENT_SIZE), study_donors.reshape(N_CELL, CELL_DEV), cell_inverse.reshape(N_CELL, CELL_DEV), validity.reshape(N_CELL, CELL_DEV)))
    return blocks.reshape(WINDOW_CELLS, LATENT_SIZE)

def projection(study_rows, frequencies, phases):
    return jnp.dot(study_rows, frequencies, preferred_element_type=jnp.float32) + phases

def reference(latents, donor_ids, study_valid_length, study_penalty_weight, frequencies, phases):
    feature_scale = math.sqrt(2.0 / FREQS)
    position = jnp.arange(WINDOW_CELLS, dtype=jnp.int32)

    def mean_features(pieces):
        study_rows, length = pieces
        validity = (position < length).astype(jnp.float32)
        cosines = jnp.cos(projection(study_rows, frequencies, phases))
        return feature_scale / length.astype(jnp.float32) * lax.optimization_barrier(jnp.sum(cosines * validity[:, None], axis=0))
    mean_feat = lax.map(mean_features, (latents, study_valid_length))
    center = lax.optimization_barrier(jnp.mean(mean_feat, axis=0))
    residual = 2.0 * feature_penalty * (mean_feat - center)

    def study_gradient(pieces):
        study_rows, study_donors, length, weight, study_residual = pieces
        validity = (position < length).astype(jnp.float32)
        drive_term = (jnp.sin(projection(study_rows, frequencies, phases)) * study_residual[None, :]).astype(jnp.bfloat16)
        backward = jnp.dot(drive_term, frequencies.T, preferred_element_type=jnp.float32)
        feature_grad = -(WINDOW_CELLS * feature_scale / length.astype(jnp.float32)) * validity[:, None] * backward
        return level_one(study_rows, study_donors, length, weight) + feature_grad
    return lax.map(study_gradient, (latents, donor_ids, study_valid_length, study_penalty_weight, residual))
```

```python
import functools
import math

import jax
import jax.numpy as jnp
from jax import lax
from jax.experimental import pallas as pl
from jax.experimental.pallas import tpu as pltpu
from jax.sharding import PartitionSpec as P

DONOR_LABELS = 16
FEATURE_PENALTY = 16.0
BLOCK = 256
DEPTH = 256
SUBLANES = 8
MIB = 1 << 20

COS_LEAD = -0.552051508388134
COS_TERMS = (-4.602194203577409, 9.359560663732573, -5.6907268683441155)
SIN_COEFS = (6.2830558, -41.33121429, 81.36681496, -74.47800249, 32.78139661)
SIN_LEAD = SIN_COEFS[4]
SIN_TERMS = tuple(c / SIN_LEAD for c in SIN_COEFS[3::-1])

VMEM_SPEC = pl.BlockSpec(memory_space=pltpu.VMEM)
SMEM_SPEC = pl.BlockSpec(memory_space=pltpu.SMEM)
ANY_SPEC = pl.BlockSpec(memory_space=pl.ANY)


def split3(x):
    hi = x.astype(jnp.bfloat16)
    rest = x - hi.astype(jnp.float32)
    mid = rest.astype(jnp.bfloat16)
    low = (rest - mid.astype(jnp.float32)).astype(jnp.bfloat16)
    return hi, mid, low


def block_start(block, cells):
    count = lax.axis_size("cell")
    return lax.rem(lax.axis_index("cell") + block, count) * cells


def valid_column(block, cells, length):
    position = lax.broadcasted_iota(jnp.int32, (cells, 1), 0) + block_start(block, cells)
    return (position < length).astype(jnp.float32)


def turn_weights_kernel(freq_hbm, phase_hbm, w_ref, freq_ref, phase_buf, sems):
    depth, width = freq_ref.shape
    start = pl.multiple_of(lax.axis_index("cell") * width, BLOCK)
    freq_copy = pltpu.make_async_copy(freq_hbm.at[:, pl.ds(start, width)], freq_ref, sems.at[0])
    phase_copy = pltpu.make_async_copy(phase_hbm.at[:, pl.ds(start, width)], phase_buf, sems.at[1])
    freq_copy.start()
    phase_copy.start()
    freq_copy.wait()
    phase_copy.wait()
    turn = 1.0 / (2.0 * math.pi)
    for part, rows in enumerate(split3(freq_ref[...].astype(jnp.float32) * turn)):
        w_ref[part * depth : (part + 1) * depth, :] = rows
    tail = DEPTH - 3 * depth
    hi, mid, low = [p.astype(jnp.float32) for p in split3(phase_buf[...] * turn)]
    row = lax.broadcasted_iota(jnp.int32, (tail, width), 0)
    rows = jnp.where(row == 0, hi, jnp.where(row == 1, mid, jnp.where(row == 2, low, 0.0)))
    w_ref[3 * depth :, :] = rows.astype(jnp.bfloat16)


def cosine_kernel(blocks, length_ref, w_ref, *refs):
    z_refs, (x_ref, out_ref, mean_ref) = refs[:blocks], refs[blocks:]
    cells, depth = z_refs[0].shape
    width = w_ref.shape[1]
    length = length_ref[0]
    for block in range(blocks):
        valid = valid_column(block, cells, length)
        rows = (z_refs[block][...].astype(jnp.float32) * valid).astype(jnp.bfloat16)
        here = pl.ds(block * cells, cells)
        for part in range(3):
            x_ref[here, part * depth : (part + 1) * depth] = rows
        lane = lax.broadcasted_iota(jnp.int32, (cells, DEPTH - 3 * depth), 1)
        x_ref[here, 3 * depth :] = jnp.where(lane < 3, valid, 0.0).astype(jnp.bfloat16)
    total_rows = blocks * cells
    scale = math.sqrt(2.0 / (width * lax.axis_size("cell")))
    per_length = 1.0 / jnp.full((1, 1), length, jnp.float32)
    a, b, c = COS_TERMS
    strip = mean_ref.shape[1]
    for offset in range(0, width, BLOCK):
        t = jnp.dot(
            x_ref[...], w_ref[:, offset : offset + BLOCK], preferred_element_type=jnp.float32
        )
        r = t - jnp.round(t)
        u = r * r
        s = r * (((u + a) * u + b) * u + c)
        squares = jnp.sum((s * s).reshape(total_rows // SUBLANES, SUBLANES, BLOCK), axis=0)
        squares = jnp.sum(squares, axis=0, keepdims=True)
        mean = scale - (2.0 * scale * COS_LEAD * COS_LEAD) * per_length * squares
        for piece in range(0, BLOCK, 128):
            row, column = divmod(offset + piece, strip)
            mean_ref[row : row + 1, column : column + 128] = mean[:, piece : piece + 128]
    mean = mean_ref[...]
    for study in range(out_ref.shape[0]):
        out_ref[study] = mean


def sine_kernel(x_ref, w_ref, *s_refs):
    cells = s_refs[0].shape[0]
    width = w_ref.shape[1]
    a, b, c, d = SIN_TERMS
    for offset in range(0, width, BLOCK):
        t = jnp.dot(
            x_ref[...], w_ref[:, offset : offset + BLOCK], preferred_element_type=jnp.float32
        )
        r = t - jnp.round(t)
        u = r * r
        s = (r * ((((u + a) * u + b) * u + c) * u + d)).astype(jnp.bfloat16)
        for block, s_ref in enumerate(s_refs):
            s_ref[:, offset : offset + BLOCK] = s[block * cells : (block + 1) * cells]


def coupling_kernel(blocks, length_ref, weight_ref, *refs):
    z_refs, donor_refs, out_ref = refs[:blocks], refs[blocks : 2 * blocks], refs[2 * blocks]
    cells, depth = out_ref.shape
    window = blocks * cells
    length = length_ref[0]
    weight = jnp.full((1, 1), weight_ref[0], jnp.float32)
    inverse_n = 1.0 / jnp.full((1, 1), length, jnp.float32)
    label = lax.broadcasted_iota(jnp.int32, (DONOR_LABELS, cells), 0)
    lane = lax.broadcasted_iota(jnp.int32, (1, cells), 1)
    members, valids = [], []
    counts = jnp.zeros((DONOR_LABELS, 1), jnp.float32)
    for block in range(blocks):
        member = (donor_refs[block][...] == label).astype(jnp.float32)
        valid = (lane + block_start(block, cells) < length).astype(jnp.float32)
        counts = counts + jnp.sum(member * valid, axis=1, keepdims=True)
        members.append(member)
        valids.append(valid)
    inverse = 1.0 / jnp.maximum(counts, 1.0)
    present = jnp.sum((counts > 0.5).astype(jnp.float32), axis=0, keepdims=True)
    row = lax.broadcasted_iota(jnp.int32, (DONOR_LABELS, cells), 0)
    own_inverse = jnp.sum(members[0] * inverse, axis=0, keepdims=True)
    left_same = jnp.concatenate(split3(members[0] * (weight * inverse * inverse)), axis=0)
    bh, bm, bl = [p.astype(jnp.float32) for p in split3(-(weight * inverse_n) * own_inverse)]
    ones = (row < 6).astype(jnp.float32)
    left_rest = jnp.where(row == 0, bh, jnp.where(row == 1, bm, jnp.where(row == 2, bl, ones)))
    left = jnp.concatenate([left_same, left_rest.astype(jnp.bfloat16)], axis=0)
    own = z_refs[0][...]
    own_wide = own.astype(jnp.float32)
    own_sq = jnp.sum(own_wide * own_wide, axis=1, keepdims=True)
    pick = jnp.ones((SUBLANES, depth), jnp.bfloat16)
    total = jnp.zeros((cells, 2 * depth), jnp.float32)
    minor = (((1,), (1,)), ((), ()))
    major = (((0,), (0,)), ((), ()))
    for block in range(blocks):
        member, valid = members[block], valids[block]
        right_inverse = jnp.sum(member * inverse, axis=0, keepdims=True)
        rest = weight * valid * inverse_n * (present * inverse_n - right_inverse)
        ch, cm, cl = [p.astype(jnp.float32) for p in split3(rest)]
        right_rest = jnp.where(
            row < 3,
            valid,
            jnp.where(row == 3, ch, jnp.where(row == 4, cm, jnp.where(row == 5, cl, 0.0))),
        ).astype(jnp.bfloat16)
        same = (member * valid).astype(jnp.bfloat16)
        right = jnp.concatenate([same, same, same, right_rest], axis=0)
        pair_weight = lax.dot_general(left, right, major, preferred_element_type=jnp.float32)
        z = z_refs[block][...]
        wide = z.astype(jnp.float32)
        square = wide * wide
        square_hi = square.astype(jnp.bfloat16)
        square_low = (square - square_hi.astype(jnp.float32)).astype(jnp.bfloat16)
        right_sq = lax.dot_general(
            pick, square_hi, minor, preferred_element_type=jnp.float32
        ) + lax.dot_general(pick, square_low, minor, preferred_element_type=jnp.float32)
        inner = lax.dot_general(own, z, minor, preferred_element_type=jnp.float32)
        squared = own_sq + right_sq[0:1] - 2.0 * inner
        coupling = pair_weight * jnp.exp(squared * (-0.5 / depth))
        hi = coupling.astype(jnp.bfloat16)
        low = (coupling - hi.astype(jnp.float32)).astype(jnp.bfloat16)
        right_rows = jnp.concatenate([z, jnp.ones((cells, depth), jnp.bfloat16)], axis=1)
        total = total + jnp.dot(hi, right_rows, preferred_element_type=jnp.float32)
        total = total + jnp.dot(low, right_rows, preferred_element_type=jnp.float32)
    row_sums = total[:, depth : depth + 1]
    own_valid = valid_column(0, cells, length)
    scale = -(2.0 * window / depth)
    out_ref[...] = scale * own_valid * (own_wide * row_sums - total[:, :depth])


def feature_part(block, length_ref, s_ref, rf_ref, window, width):
    cells = s_ref.shape[0]
    depth = rf_ref.shape[0] // 2
    both = lax.dot_general(
        s_ref[...], rf_ref[...], (((1,), (1,)), ((), ())), preferred_element_type=jnp.float32
    )
    scale = SIN_LEAD * window * math.sqrt(2.0 / (width * lax.axis_size("cell")))
    length = length_ref[0]
    factor = -scale / jnp.full((1, 1), length, jnp.float32)
    return factor * valid_column(block, cells, length) * (both[:, :depth] + both[:, depth:])


def residual_kernel(block, window, length_ref, gathered_ref, mean_ref, freq_ref, s_ref, out_ref, rf_ref):
    studies, _, strip = gathered_ref.shape
    depth, width = freq_ref.shape
    center = gathered_ref[0]
    for study in range(1, studies):
        center = center + gathered_ref[study]
    residual = (2.0 * FEATURE_PENALTY) * (mean_ref[0] - center * (1.0 / studies))
    for row in range(SUBLANES):
        here = slice(row * strip, (row + 1) * strip)
        rows = freq_ref[:, here].astype(jnp.float32) * residual[row : row + 1]
        hi = rows.astype(jnp.bfloat16)
        rf_ref[:depth, here] = hi
        rf_ref[depth:, here] = (rows - hi.astype(jnp.float32)).astype(jnp.bfloat16)
    out_ref[...] = feature_part(block, length_ref, s_ref, rf_ref, window, width)


def own_kernel(window, length_ref, s_ref, rf_ref, base_ref, out_ref):
    width = rf_ref.shape[1]
    out_ref[...] = base_ref[...] + feature_part(0, length_ref, s_ref, rf_ref, window, width)


def call(kernel, out_shape, in_specs, name, flops, transcendentals=0, size=0, scratch=(), vmem=32):
    several = isinstance(out_shape, (list, tuple))
    return pl.pallas_call(
        kernel,
        out_shape=out_shape,
        in_specs=in_specs,
        out_specs=[VMEM_SPEC] * len(out_shape) if several else VMEM_SPEC,
        scratch_shapes=list(scratch),
        compiler_params=pltpu.CompilerParams(vmem_limit_bytes=vmem * MIB),
        cost_estimate=pl.CostEstimate(
            flops=int(flops), bytes_accessed=int(size), transcendentals=int(transcendentals)
        ),
        name=name,
    )


def rotated(x, shift):
    count = lax.axis_size("cell")
    return lax.ppermute(x, "cell", [((i + shift) % count, i) for i in range(count)])


def on_device(latents, donor_ids, study_valid_length, study_penalty_weight, frequencies, phases):
    own = latents[0]
    cells, depth = own.shape
    blocks = lax.axis_size("cell")
    studies = lax.axis_size("study")
    features = frequencies.shape[1]
    width = features // blocks
    window = blocks * cells
    strip = width // SUBLANES
    f32, bf16 = jnp.float32, jnp.bfloat16
    shape = jax.ShapeDtypeStruct
    pairs = window * width

    rows = [own] + [rotated(own, k) for k in range(1, blocks)]
    donors = [donor_ids] + [rotated(donor_ids, k) for k in range(1, blocks)]

    turn_weights, freq_part = call(
        turn_weights_kernel,
        [shape((DEPTH, width), bf16), shape((depth, width), bf16)],
        [ANY_SPEC, ANY_SPEC],
        "turn_weights",
        flops=20 * depth * width,
        size=4 * depth * width,
        scratch=[pltpu.VMEM((1, width), f32), pltpu.SemaphoreType.DMA((2,))],
    )(frequencies, phases.reshape(1, features))

    x, copies = call(
        functools.partial(cosine_kernel, blocks),
        [shape((window, DEPTH), bf16), shape((studies, SUBLANES, strip), f32)],
        [SMEM_SPEC] + [VMEM_SPEC] * (1 + blocks),
        "cosine_sums",
        flops=2 * DEPTH * pairs + 12 * pairs,
        size=2 * DEPTH * width,
        scratch=[pltpu.VMEM((SUBLANES, strip), f32)],
    )(study_valid_length, turn_weights, *rows)

    gathered = lax.all_to_all(copies, "study", 0, 0, tiled=True)

    sines = call(
        sine_kernel,
        [shape((cells, width), bf16)] * blocks,
        [VMEM_SPEC] * 2,
        "sines",
        flops=2 * DEPTH * pairs + 12 * pairs,
        size=2 * pairs,
    )(x, turn_weights)
    base = call(
        functools.partial(coupling_kernel, blocks),
        shape((cells, depth), f32),
        [SMEM_SPEC] * 2 + [VMEM_SPEC] * (2 * blocks),
        "coupling",
        flops=2 * cells * window * (3 * depth),
        transcendentals=cells * window,
        size=4 * cells * depth,
    )(study_valid_length, study_penalty_weight, *rows, *donors)

    out = None
    residual_freq = None
    for block in range(1, blocks):
        if residual_freq is None:
            part, residual_freq = call(
                functools.partial(residual_kernel, block, window),
                [shape((cells, depth), f32), shape((2 * depth, width), bf16)],
                [SMEM_SPEC] + [VMEM_SPEC] * 4,
                "residual_part",
                flops=2 * cells * width * depth,
                size=2 * cells * width,
            )(study_valid_length, gathered, copies[:1], freq_part, sines[block])
        else:
            part = call(
                functools.partial(other_kernel, block, window),
                shape((cells, depth), f32),
                [SMEM_SPEC] + [VMEM_SPEC] * 2,
                "other_part",
                flops=2 * cells * width * depth,
                size=2 * cells * width,
            )(study_valid_length, sines[block], residual_freq)
        sent = rotated(part, blocks - block)
        out = sent if out is None else out + sent
    own_part = call(
        functools.partial(own_kernel, window),
        shape((cells, depth), f32),
        [SMEM_SPEC] + [VMEM_SPEC] * 3,
        "own_part",
        flops=2 * cells * width * depth,
        size=2 * cells * width,
    )(study_valid_length, sines[0], residual_freq, base)
    return (own_part + out)[None]


def other_kernel(block, window, length_ref, s_ref, rf_ref, out_ref):
    width = rf_ref.shape[1]
    out_ref[...] = feature_part(block, length_ref, s_ref, rf_ref, window, width)


def solution(mesh):
    in_specs = (P("study", "cell", None), P("study", "cell"), P("study"), P("study"), P(), P())
    out_specs = P("study", "cell", None)
    return jax.shard_map(
        on_device, mesh=mesh, in_specs=in_specs, out_specs=out_specs, check_vma=False
    )
```

```python
import functools
import math

import jax
import jax.numpy as jnp
from jax import lax
from jax.experimental import pallas as pl
from jax.experimental.pallas import tpu as pltpu
from jax.sharding import PartitionSpec as P

DONOR_LABELS = 16
FEATURE_PENALTY = 16.0
BLOCK = 256
PAIR = 128
SUBLANES = 8
MIB = 1 << 20

COS_LEAD = -0.552051508388134
COS_TERMS = (-4.602194203577409, 9.359560663732573, -5.6907268683441155)
SIN_LEAD = 2.0 * COS_LEAD * abs(COS_LEAD)

VMEM_SPEC = pl.BlockSpec(memory_space=pltpu.VMEM)
HBM_SPEC = pl.BlockSpec(memory_space=pltpu.HBM)


def split3(x):
    hi = x.astype(jnp.bfloat16)
    rest = x - hi.astype(jnp.float32)
    mid = rest.astype(jnp.bfloat16)
    low = (rest - mid.astype(jnp.float32)).astype(jnp.bfloat16)
    return hi, mid, low


def block_start(block, cells):
    count = lax.axis_size("cell")
    return lax.rem(lax.axis_index("cell") + block, count) * cells


def valid_row(block, cells, length):
    position = lax.broadcasted_iota(jnp.int32, (1, cells), 1) + block_start(block, cells)
    return (position.astype(jnp.float32) < length).astype(jnp.float32)


def feature_scale(width):
    return math.sqrt(2.0 / (width * lax.axis_size("cell")))


def store_rows(x_ref, z, valid):
    depth, cells = z.shape
    z = z.astype(jnp.float32) * valid
    tail = 2 * PAIR - 3 * depth
    ones = jnp.where(lax.broadcasted_iota(jnp.int32, (tail, cells), 0) < 3, valid, 0.0)
    x_ref[:, :PAIR] = jnp.concatenate([z, z], axis=0).T.astype(jnp.bfloat16)
    x_ref[:, PAIR:] = jnp.concatenate([z, ones], axis=0).T.astype(jnp.bfloat16)


def setup_kernel(const_ref, freq_hbm, phase_hbm, z_hbm, w_ref, freq_ref, z_ref, x_ref, phase_buf, sems):
    depth, width = freq_ref.shape
    start = pl.multiple_of(lax.axis_index("cell") * width, BLOCK)
    copies = [
        pltpu.make_async_copy(source, target, sems.at[i])
        for i, (source, target) in enumerate(
            [
                (z_hbm, z_ref),
                (phase_hbm.at[:, pl.ds(start, width)], phase_buf),
                (freq_hbm.at[:, pl.ds(start, width)], freq_ref),
            ]
        )
    ]
    for copy in copies:
        copy.start()
    copies[0].wait()
    length = const_ref[0:1, 0:1]
    store_rows(x_ref, z_ref[...], valid_row(0, z_ref.shape[1], length))
    for copy in copies[1:]:
        copy.wait()
    turn = 1.0 / (2.0 * math.pi)
    for part, rows in enumerate(split3(freq_ref[...].astype(jnp.float32) * turn)):
        w_ref[part * depth : (part + 1) * depth, :] = rows
    tail = 2 * PAIR - 3 * depth
    hi, mid, low = [p.astype(jnp.float32) for p in split3(phase_buf[...] * turn)]
    row = lax.broadcasted_iota(jnp.int32, (tail, width), 0)
    rows = jnp.where(row == 0, hi, jnp.where(row == 1, mid, jnp.where(row == 2, low, 0.0)))
    w_ref[3 * depth :, :] = rows.astype(jnp.bfloat16)


def cosine_kernel(blocks, const_ref, w_ref, x_own_ref, *refs):
    z_refs = refs[: blocks - 1]
    s_refs = refs[blocks - 1 : 2 * blocks - 1]
    mean_ref = refs[2 * blocks - 1]
    x_refs = [x_own_ref, *refs[2 * blocks :]]
    cells, width = s_refs[0].shape
    length = const_ref[0:1, 0:1]
    for block in range(1, blocks):
        store_rows(x_refs[block], z_refs[block - 1][...], valid_row(block, cells, length))
    scale = feature_scale(width)
    per_length = 1.0 / length
    a, b, c = COS_TERMS
    strip = mean_ref.shape[1]
    for offset in range(0, width, BLOCK):
        here = slice(offset, offset + BLOCK)
        squares = jnp.zeros((SUBLANES, BLOCK), jnp.float32)
        for x_ref, s_ref in zip(x_refs, s_refs):
            t = jnp.dot(x_ref[...], w_ref[:, here], preferred_element_type=jnp.float32)
            r = t - jnp.round(t)
            u = r * r
            s = r * (((u + a) * u + b) * u + c)
            s_ref[:, here] = s
            squares += jnp.sum((s * s).reshape(cells // SUBLANES, SUBLANES, BLOCK), axis=0)
        squares = jnp.sum(squares, axis=0, keepdims=True)
        mean = scale - (2.0 * scale * COS_LEAD * COS_LEAD) * per_length * squares
        for piece in range(0, BLOCK, 128):
            row, column = divmod(offset + piece, strip)
            mean_ref[row : row + 1, column : column + 128] = mean[:, piece : piece + 128]


def sine_kernel(blocks, *refs):
    top = (1.0 + 2e-6) / (COS_LEAD * COS_LEAD)
    cells, width = refs[0].shape
    for s_ref, out_ref in zip(refs[:blocks], refs[blocks:]):
        for offset in range(0, width, BLOCK):
            here = slice(offset, offset + BLOCK)
            s = s_ref[:, here]
            rest = top - s * s
            out_ref[:, here] = (s * (rest * lax.rsqrt(rest))).astype(jnp.bfloat16)


def coupling_kernel(blocks, const_ref, *refs):
    z_refs, donor_refs, out_ref = refs[:blocks], refs[blocks : 2 * blocks], refs[2 * blocks]
    depth, cells = out_ref.shape
    window = blocks * cells
    length = const_ref[0:1, 0:1]
    weight = const_ref[1:2, 0:1]
    inverse_n = 1.0 / length
    label = lax.broadcasted_iota(jnp.int32, (DONOR_LABELS, cells), 0)
    members, valids = [], []
    counts = jnp.zeros((DONOR_LABELS, 1), jnp.float32)
    for block in range(blocks):
        member = (donor_refs[block][...] == label).astype(jnp.float32)
        valid = valid_row(block, cells, length)
        counts = counts + jnp.sum(member * valid, axis=1, keepdims=True)
        members.append(member)
        valids.append(valid)
    inverse = 1.0 / jnp.maximum(counts, 1.0)
    present = jnp.sum((counts > 0.5).astype(jnp.float32), axis=0, keepdims=True)
    row = lax.broadcasted_iota(jnp.int32, (DONOR_LABELS, cells), 0)
    own_inverse = jnp.sum(members[0] * inverse, axis=0, keepdims=True)
    left_same = jnp.concatenate(split3(members[0] * (weight * inverse * inverse)), axis=0)
    bh, bm, bl = [p.astype(jnp.float32) for p in split3(-(weight * inverse_n) * own_inverse)]
    ones = (row < 6).astype(jnp.float32)
    left_rest = jnp.where(row == 0, bh, jnp.where(row == 1, bm, jnp.where(row == 2, bl, ones)))
    left = jnp.concatenate([left_same, left_rest.astype(jnp.bfloat16)], axis=0)
    own = z_refs[0][...]
    own_wide = own.astype(jnp.float32)
    own_sq = jnp.sum(own_wide * own_wide, axis=0, keepdims=True)
    total = jnp.zeros((cells, PAIR), jnp.float32)
    minor = (((1,), (1,)), ((), ()))
    major = (((0,), (0,)), ((), ()))
    own_column = jnp.broadcast_to(own_sq, (PAIR, cells)).T[:, 0:1]
    for block in range(blocks):
        member, valid = members[block], valids[block]
        right_inverse = jnp.sum(member * inverse, axis=0, keepdims=True)
        rest = weight * valid * inverse_n * (present * inverse_n - right_inverse)
        ch, cm, cl = [p.astype(jnp.float32) for p in split3(rest)]
        right_rest = jnp.where(
            row < 3,
            valid,
            jnp.where(row == 3, ch, jnp.where(row == 4, cm, jnp.where(row == 5, cl, 0.0))),
        ).astype(jnp.bfloat16)
        same = (member * valid).astype(jnp.bfloat16)
        right = jnp.concatenate([same, same, same, right_rest], axis=0)
        pair_weight = lax.dot_general(left, right, major, preferred_element_type=jnp.float32)
        z = z_refs[block][...]
        wide = z.astype(jnp.float32)
        right_sq = jnp.sum(wide * wide, axis=0, keepdims=True)
        inner = lax.dot_general(own, z, major, preferred_element_type=jnp.float32)
        squared = own_column + right_sq - 2.0 * inner
        coupling = pair_weight * jnp.exp(squared * (-0.5 / depth))
        hi = coupling.astype(jnp.bfloat16)
        low = (coupling - hi.astype(jnp.float32)).astype(jnp.bfloat16)
        right_rows = jnp.concatenate([z, jnp.ones((PAIR - depth, cells), jnp.bfloat16)], axis=0)
        for part in (hi, low):
            total = total + lax.dot_general(
                part, right_rows, minor, preferred_element_type=jnp.float32
            )
    total = total.T
    scale = -(2.0 * window / depth)
    own_valid = valid_row(0, cells, length)
    out_ref[...] = scale * own_valid * (own_wide * total[depth : depth + 1] - total[:depth])


def feature_part(block, const_ref, s_ref, rf_ref, window):
    cells, width = s_ref.shape
    depth = rf_ref.shape[0] // 2
    both = lax.dot_general(
        s_ref[...], rf_ref[...], (((1,), (1,)), ((), ())), preferred_element_type=jnp.float32
    ).T
    length = const_ref[0:1, 0:1]
    factor = -(SIN_LEAD * window * feature_scale(width)) / length
    return factor * valid_row(block, cells, length) * (both[:depth] + both[depth:])


def residual_kernel(block, window, const_ref, sum_ref, mean_ref, freq_ref, s_ref, out_ref, rf_ref):
    strip = sum_ref.shape[1]
    depth = freq_ref.shape[0]
    center = sum_ref[...] * (1.0 / lax.axis_size("study"))
    residual = (2.0 * FEATURE_PENALTY) * (mean_ref[...] - center)
    for row in range(SUBLANES):
        here = slice(row * strip, (row + 1) * strip)
        rows = freq_ref[:, here].astype(jnp.float32) * residual[row : row + 1]
        hi = rows.astype(jnp.bfloat16)
        rf_ref[:depth, here] = hi
        rf_ref[depth:, here] = (rows - hi.astype(jnp.float32)).astype(jnp.bfloat16)
    out_ref[...] = feature_part(block, const_ref, s_ref, rf_ref, window)


def other_kernel(block, window, const_ref, s_ref, rf_ref, out_ref):
    out_ref[...] = feature_part(block, const_ref, s_ref, rf_ref, window)


def own_kernel(window, const_ref, s_ref, rf_ref, base_ref, out_ref):
    out_ref[...] = base_ref[...] + feature_part(0, const_ref, s_ref, rf_ref, window)


def call(kernel, out_shape, name, flops, transcendentals=0, size=0, scratch=(), vmem=8, in_specs=None):
    several = isinstance(out_shape, (list, tuple))

    def run(*operands):
        return pl.pallas_call(
            kernel,
            out_shape=out_shape,
            in_specs=in_specs or [VMEM_SPEC] * len(operands),
            out_specs=[VMEM_SPEC] * len(out_shape) if several else VMEM_SPEC,
            scratch_shapes=list(scratch),
            compiler_params=pltpu.CompilerParams(vmem_limit_bytes=vmem * MIB),
            cost_estimate=pl.CostEstimate(
                flops=int(flops), bytes_accessed=int(size), transcendentals=int(transcendentals)
            ),
            name=name,
        )(*operands)

    return run


def rotated(x, shift):
    count = lax.axis_size("cell")
    return lax.ppermute(x, "cell", [((i + shift) % count, i) for i in range(count)])


def digits(count):
    radices = []
    while count > 1:
        radix = next(r for r in (4, 2, *range(3, count + 1)) if count % r == 0)
        radices.append(radix)
        count //= radix
    return radices


def swapped(x, stride, radix):
    count = lax.axis_size("study")

    def partner(i, k):
        digit = i // stride % radix
        other = digit ^ k if radix & (radix - 1) == 0 else (digit + k) % radix
        return i + (other - digit) * stride

    return [
        lax.ppermute(x, "study", [(i, partner(i, k)) for i in range(count)])
        for k in range(1, radix)
    ]


def on_device(latents, donor_ids, study_valid_length, study_penalty_weight, frequencies, phases):
    own = jnp.swapaxes(latents[0], 0, 1)
    depth, cells = own.shape
    blocks = lax.axis_size("cell")
    studies = lax.axis_size("study")
    features = frequencies.shape[1]
    width = features // blocks
    window = blocks * cells
    strip = width // SUBLANES
    f32, bf16 = jnp.float32, jnp.bfloat16
    shape = jax.ShapeDtypeStruct
    pairs = window * width

    others = [rotated(own, k) for k in range(1, blocks)]
    donors = [donor_ids] + [rotated(donor_ids, k) for k in range(1, blocks)]

    consts = jnp.broadcast_to(
        jnp.stack([study_valid_length.astype(f32), study_penalty_weight]), (2, 128)
    )
    in_hbm = [
        pltpu.with_memory_space_constraint(operand, pltpu.HBM)
        for operand in (frequencies, phases.reshape(1, features), own)
    ]
    turn_weights, freq_part, own, x_own = call(
        setup_kernel,
        [
            shape((2 * PAIR, width), bf16),
            shape((depth, width), bf16),
            shape((depth, cells), bf16),
            shape((cells, 2 * PAIR), bf16),
        ],
        "setup",
        flops=20 * depth * width,
        size=4 * depth * width,
        scratch=[pltpu.VMEM((1, width), f32), pltpu.SemaphoreType.DMA((3,))],
        in_specs=[VMEM_SPEC] + [HBM_SPEC] * 3,
    )(consts, *in_hbm)

    *halves, mean = call(
        functools.partial(cosine_kernel, blocks),
        [shape((cells, width), f32)] * blocks + [shape((SUBLANES, strip), f32)],
        "cosine_sums",
        flops=4 * PAIR * pairs + 12 * pairs,
        size=4 * PAIR * width,
        scratch=[pltpu.VMEM((cells, 2 * PAIR), bf16)] * (blocks - 1),
    )(consts, turn_weights, x_own, *others)

    def couplings(z_blocks):
        return call(
            functools.partial(coupling_kernel, blocks),
            shape((depth, cells), f32),
            "coupling",
            flops=2 * cells * window * (3 * depth),
            transcendentals=cells * window,
            size=4 * cells * depth,
        )(consts, *z_blocks, *donors)

    center, base, stride = mean, None, 1
    for radix in digits(studies):
        parts = swapped(center, stride, radix)
        stride *= radix
        if base is None:
            base = couplings([own, *others])
            center = sum(parts, center)
            center, base, *halves = lax.optimization_barrier((center, base, *halves))
        else:
            center = sum(parts, center)
    if base is None:
        base = couplings([own, *others])

    sines = call(
        functools.partial(sine_kernel, blocks),
        [shape((cells, width), bf16)] * blocks,
        "sines",
        flops=12 * pairs,
        transcendentals=pairs,
        size=6 * pairs,
    )(*halves)

    out, residual_freq = None, None
    part_shape = shape((depth, cells), f32)
    cost = dict(flops=2 * cells * width * depth, size=2 * cells * width)
    for block in range(1, blocks):
        if residual_freq is None:
            part, residual_freq = call(
                functools.partial(residual_kernel, block, window),
                [part_shape, shape((2 * depth, width), bf16)],
                "residual_part",
                **cost,
            )(consts, center, mean, freq_part, sines[block])
        else:
            part = call(
                functools.partial(other_kernel, block, window), part_shape, "other_part", **cost
            )(consts, sines[block], residual_freq)
        sent = rotated(part, blocks - block)
        out = sent if out is None else out + sent
    own_part = call(functools.partial(own_kernel, window), part_shape, "own_part", **cost)(
        consts, sines[0], residual_freq, base
    )
    return jnp.swapaxes(own_part + out, 0, 1)[None]


def solution(mesh):
    in_specs = (P("study", "cell", None), P("study", "cell"), P("study"), P("study"), P(), P())
    out_specs = P("study", "cell", None)
    return jax.shard_map(
        on_device, mesh=mesh, in_specs=in_specs, out_specs=out_specs, check_vma=False
    )
```

```python
import functools
import math

import jax
import jax.numpy as jnp
from jax import lax
from jax.experimental import pallas as pl
from jax.experimental.pallas import tpu as pltpu
from jax.sharding import PartitionSpec as P

DONOR_LABELS = 16
FEATURE_PENALTY = 16.0
BLOCK = 256
PAIR = 128
SUBLANES = 8
MIB = 1 << 20

COS_LEAD = -0.552051508388134
COS_TERMS = (-4.602194203577409, 9.359560663732573, -5.6907268683441155)
SIN_LEAD = 2.0 * COS_LEAD * abs(COS_LEAD)

VMEM_SPEC = pl.BlockSpec(memory_space=pltpu.VMEM)
SMEM_SPEC = pl.BlockSpec(memory_space=pltpu.SMEM)
HBM_SPEC = pl.BlockSpec(memory_space=pltpu.HBM)


def split3(x):
    hi = x.astype(jnp.bfloat16)
    rest = x - hi.astype(jnp.float32)
    mid = rest.astype(jnp.bfloat16)
    low = (rest - mid.astype(jnp.float32)).astype(jnp.bfloat16)
    return hi, mid, low


def block_start(block, cells):
    count = lax.axis_size("cell")
    return lax.rem(lax.axis_index("cell") + block, count) * cells


def valid_row(block, cells, length):
    position = lax.broadcasted_iota(jnp.int32, (1, cells), 1) + block_start(block, cells)
    return (position.astype(jnp.float32) < length).astype(jnp.float32)


def feature_scale(width):
    return math.sqrt(2.0 / (width * lax.axis_size("cell")))


def store_rows(x_ref, z, valid):
    depth, cells = z.shape
    z = z.astype(jnp.float32) * valid
    tail = 2 * PAIR - 3 * depth
    ones = jnp.where(lax.broadcasted_iota(jnp.int32, (tail, cells), 0) < 3, valid, 0.0)
    x_ref[:, :PAIR] = jnp.concatenate([z, z], axis=0).T.astype(jnp.bfloat16)
    x_ref[:, PAIR:] = jnp.concatenate([z, ones], axis=0).T.astype(jnp.bfloat16)


def setup_kernel(length_ref, freq_hbm, phase_hbm, z_hbm, w_ref, freq_ref, z_ref, x_ref, const_ref, phase_buf, sems):
    depth, width = freq_ref.shape
    start = pl.multiple_of(lax.axis_index("cell") * width, BLOCK)
    copies = [
        pltpu.make_async_copy(source, target, sems.at[i])
        for i, (source, target) in enumerate(
            [
                (z_hbm, z_ref),
                (phase_hbm.at[:, pl.ds(start, width)], phase_buf),
                (freq_hbm.at[:, pl.ds(start, width)], freq_ref),
            ]
        )
    ]
    for copy in copies:
        copy.start()
    length = jnp.full((1, 1), length_ref[0], jnp.int32).astype(jnp.float32)
    const_ref[...] = jnp.broadcast_to(length, const_ref.shape)
    copies[0].wait()
    store_rows(x_ref, z_ref[...], valid_row(0, z_ref.shape[1], length))
    for copy in copies[1:]:
        copy.wait()
    turn = 1.0 / (2.0 * math.pi)
    for part, rows in enumerate(split3(freq_ref[...].astype(jnp.float32) * turn)):
        w_ref[part * depth : (part + 1) * depth, :] = rows
    tail = 2 * PAIR - 3 * depth
    hi, mid, low = [p.astype(jnp.float32) for p in split3(phase_buf[...] * turn)]
    row = lax.broadcasted_iota(jnp.int32, (tail, width), 0)
    rows = jnp.where(row == 0, hi, jnp.where(row == 1, mid, jnp.where(row == 2, low, 0.0)))
    w_ref[3 * depth :, :] = rows.astype(jnp.bfloat16)


def cosine_kernel(blocks, const_ref, w_ref, x_own_ref, *refs):
    z_refs = refs[: blocks - 1]
    s_refs = refs[blocks - 1 : 2 * blocks - 1]
    mean_ref = refs[2 * blocks - 1]
    x_refs = [x_own_ref, *refs[2 * blocks :]]
    cells, width = s_refs[0].shape
    length = const_ref[0:1, 0:1]
    for block in range(1, blocks):
        store_rows(x_refs[block], z_refs[block - 1][...], valid_row(block, cells, length))
    scale = feature_scale(width)
    per_length = 1.0 / length
    a, b, c = COS_TERMS
    strip = mean_ref.shape[1]
    for offset in range(0, width, BLOCK):
        here = slice(offset, offset + BLOCK)
        squares = jnp.zeros((SUBLANES, BLOCK), jnp.float32)
        for x_ref, s_ref in zip(x_refs, s_refs):
            t = jnp.dot(x_ref[...], w_ref[:, here], preferred_element_type=jnp.float32)
            r = t - jnp.round(t)
            u = r * r
            s = r * (((u + a) * u + b) * u + c)
            s_ref[:, here] = s
            squares += jnp.sum((s * s).reshape(cells // SUBLANES, SUBLANES, BLOCK), axis=0)
        squares = jnp.sum(squares, axis=0, keepdims=True)
        mean = scale - (2.0 * scale * COS_LEAD * COS_LEAD) * per_length * squares
        for piece in range(0, BLOCK, 128):
            row, column = divmod(offset + piece, strip)
            mean_ref[row : row + 1, column : column + 128] = mean[:, piece : piece + 128]


def sine_kernel(blocks, *refs):
    top = (1.0 + 2e-6) / (COS_LEAD * COS_LEAD)
    cells, width = refs[0].shape
    for s_ref, out_ref in zip(refs[:blocks], refs[blocks:]):
        for offset in range(0, width, BLOCK):
            here = slice(offset, offset + BLOCK)
            s = s_ref[:, here]
            rest = top - s * s
            out_ref[:, here] = (s * (rest * lax.rsqrt(rest))).astype(jnp.bfloat16)


def stacked(rows, cells):
    index = lax.broadcasted_iota(jnp.int32, (DONOR_LABELS, cells), 0)
    total = jnp.zeros((DONOR_LABELS, cells), jnp.float32)
    for k, row in enumerate(rows):
        if row is not None:
            total = jnp.where(index == k, row, total)
    return total.astype(jnp.bfloat16)


def coupling_kernel(blocks, owner, weight_ref, const_ref, *refs):
    z_refs, donor_refs, out_refs = refs[:blocks], refs[blocks : 2 * blocks], refs[2 * blocks :]
    depth, cells = out_refs[0].shape
    window = blocks * cells
    f32, bf16 = jnp.float32, jnp.bfloat16

    def compute():
        length = const_ref[0:1, 0:1]
        inverse_n = 1.0 / length
        label = lax.broadcasted_iota(jnp.int32, (DONOR_LABELS, cells), 0)
        members = [(ref[...] == label).astype(f32) for ref in donor_refs]
        valids = [valid_row(block, cells, length) for block in range(blocks)]
        counts = sum(
            jnp.sum(member * valid, axis=1, keepdims=True)
            for member, valid in zip(members, valids)
        )
        inverse = 1.0 / jnp.maximum(counts, 1.0)
        present = jnp.sum((counts > 0.5).astype(f32), axis=0, keepdims=True)
        one = jnp.ones((1, 1), f32)
        wides = [ref[...].astype(f32) for ref in z_refs]
        norms = [
            [p.astype(f32) for p in split3(-0.5 * jnp.sum(z * z, axis=0, keepdims=True))]
            for z in wides
        ]
        shares = [
            inverse_n * jnp.sum(member * inverse, axis=0, keepdims=True) for member in members
        ]
        same_zero = jnp.zeros((3 * DONOR_LABELS, cells), bf16)
        z_zero = jnp.zeros((depth, cells), bf16)
        rights = []
        for target in range(len(out_refs)):
            rest = [p.astype(f32) for p in split3(present * inverse_n * inverse_n - shares[target])]
            member = members[target].astype(bf16)
            exponent = [z_refs[target][...], stacked([one] * 3 + norms[target], cells), same_zero]
            pair = [z_zero, stacked([None] * 6 + [one] * 3 + rest, cells), member, member, member]
            rights.append(
                jnp.concatenate(
                    [jnp.concatenate(exponent, axis=0), jnp.concatenate(pair, axis=0)], axis=1
                )
            )
        totals = [jnp.zeros((PAIR, cells), f32) for _ in out_refs]
        for source in range(blocks):
            valid = valids[source]
            z = z_refs[source][...]
            minus = [p.astype(f32) for p in split3(-shares[source] * valid)]
            left = jnp.concatenate(
                [
                    z,
                    stacked(norms[source] + [one] * 3 + minus + [valid] * 3, cells),
                    *split3(members[source] * (inverse * inverse) * valid),
                ],
                axis=0,
            ).astype(f32).T.astype(bf16)
            rows = jnp.concatenate([z, jnp.ones((PAIR - depth, cells), bf16)], axis=0)
            for target, right in enumerate(rights):
                both = jnp.dot(left, right, preferred_element_type=f32)
                coupling = both[:, cells:] * jnp.exp2(both[:, :cells] * (math.log2(math.e) / depth))
                hi = coupling.astype(bf16)
                low = (coupling - hi.astype(f32)).astype(bf16)
                totals[target] += jnp.dot(rows, hi, preferred_element_type=f32)
                totals[target] += jnp.dot(rows, low, preferred_element_type=f32)
        scale = -(2.0 * window / depth) * jnp.full((1, 1), weight_ref[0], f32)
        for target, out_ref in enumerate(out_refs):
            total = totals[target]
            gradient = wides[target] * total[depth : depth + 1] - total[:depth]
            out_ref[...] = scale * valids[target] * gradient

    if owner is None:
        compute()
        return
    pl.when(lax.axis_index("cell") == owner)(compute)

    @pl.when(lax.axis_index("cell") != owner)
    def _():
        for out_ref in out_refs:
            out_ref[...] = jnp.zeros((depth, cells), f32)


def feature_part(block, const_ref, s_ref, rf_ref, window):
    cells, width = s_ref.shape
    depth = rf_ref.shape[0] // 2
    both = lax.dot_general(
        s_ref[...], rf_ref[...], (((1,), (1,)), ((), ())), preferred_element_type=jnp.float32
    ).T
    length = const_ref[0:1, 0:1]
    factor = -(SIN_LEAD * window * feature_scale(width)) / length
    return factor * valid_row(block, cells, length) * (both[:depth] + both[depth:])


def residual_kernel(block, window, const_ref, sum_ref, mean_ref, freq_ref, s_ref, *refs):
    *base_refs, out_ref, rf_ref = refs
    strip = sum_ref.shape[1]
    depth = freq_ref.shape[0]
    center = sum_ref[...] * (1.0 / lax.axis_size("study"))
    residual = (2.0 * FEATURE_PENALTY) * (mean_ref[...] - center)
    for row in range(SUBLANES):
        here = slice(row * strip, (row + 1) * strip)
        rows = freq_ref[:, here].astype(jnp.float32) * residual[row : row + 1]
        hi = rows.astype(jnp.bfloat16)
        rf_ref[:depth, here] = hi
        rf_ref[depth:, here] = (rows - hi.astype(jnp.float32)).astype(jnp.bfloat16)
    part_kernel(block, window, const_ref, s_ref, rf_ref, *base_refs, out_ref)


def part_kernel(block, window, const_ref, s_ref, rf_ref, *refs):
    *base_refs, out_ref = refs
    part = feature_part(block, const_ref, s_ref, rf_ref, window)
    out_ref[...] = sum((ref[...] for ref in base_refs), part)


def call(kernel, out_shape, name, flops, transcendentals=0, size=0, scratch=(), vmem=8, in_specs=None):
    several = isinstance(out_shape, (list, tuple))

    def run(*operands):
        return pl.pallas_call(
            kernel,
            out_shape=out_shape,
            in_specs=in_specs or [VMEM_SPEC] * len(operands),
            out_specs=[VMEM_SPEC] * len(out_shape) if several else VMEM_SPEC,
            scratch_shapes=list(scratch),
            compiler_params=pltpu.CompilerParams(vmem_limit_bytes=vmem * MIB),
            cost_estimate=pl.CostEstimate(
                flops=int(flops), bytes_accessed=int(size), transcendentals=int(transcendentals)
            ),
            name=name,
        )(*operands)

    return run


def in_hbm(x):
    return pltpu.with_memory_space_constraint(x, pltpu.HBM)


def rotated(x, shift):
    count = lax.axis_size("cell")
    return lax.ppermute(x, "cell", [((i + shift) % count, i) for i in range(count)])


def digits(count):
    radices = []
    while count > 1:
        radix = next(r for r in (4, 2, *range(3, count + 1)) if count % r == 0)
        radices.append(radix)
        count //= radix
    return radices


def swapped(x, stride, radix):
    count = lax.axis_size("study")

    def partner(i, k):
        digit = i // stride % radix
        other = digit ^ k if radix & (radix - 1) == 0 else (digit + k) % radix
        return i + (other - digit) * stride

    return [
        lax.ppermute(x, "study", [(i, partner(i, k)) for i in range(count)])
        for k in range(radix - 1, 0, -1)
    ]


def on_device(latents, donor_ids, study_valid_length, study_penalty_weight, frequencies, phases):
    own = jnp.swapaxes(latents[0], 0, 1)
    depth, cells = own.shape
    blocks = lax.axis_size("cell")
    studies = lax.axis_size("study")
    features = frequencies.shape[1]
    width = features // blocks
    window = blocks * cells
    strip = width // SUBLANES
    f32, bf16 = jnp.float32, jnp.bfloat16
    shape = jax.ShapeDtypeStruct
    pairs = window * width

    others = [rotated(own, k) for k in range(1, blocks)]
    donors = [donor_ids] + [rotated(donor_ids, k) for k in range(1, blocks)]

    turn_weights, freq_part, own, x_own, consts = call(
        setup_kernel,
        [
            shape((2 * PAIR, width), bf16),
            shape((depth, width), bf16),
            shape((depth, cells), bf16),
            shape((cells, 2 * PAIR), bf16),
            shape((1, 128), f32),
        ],
        "setup",
        flops=20 * depth * width,
        size=4 * depth * width,
        scratch=[pltpu.VMEM((1, width), f32), pltpu.SemaphoreType.DMA((3,))],
        in_specs=[SMEM_SPEC] + [HBM_SPEC] * 3,
    )(
        study_valid_length,
        *[in_hbm(x) for x in (frequencies, phases.reshape(1, features), own)],
    )

    *halves, mean = call(
        functools.partial(cosine_kernel, blocks),
        [shape((cells, width), f32)] * blocks + [shape((SUBLANES, strip), f32)],
        "cosine_sums",
        flops=4 * PAIR * pairs + 12 * pairs,
        size=4 * PAIR * width,
        scratch=[pltpu.VMEM((cells, 2 * PAIR), bf16)] * (blocks - 1),
    )(consts, turn_weights, x_own, *others)

    def couplings():
        outputs, owner = (2, 1) if blocks == 2 else (1, None)
        return call(
            functools.partial(coupling_kernel, blocks, owner),
            [shape((depth, cells), f32)] * outputs,
            "coupling",
            flops=2 * cells * window * (3 * depth),
            transcendentals=cells * window,
            size=4 * cells * depth,
            in_specs=[SMEM_SPEC] + [VMEM_SPEC] * (1 + 2 * blocks),
        )(study_penalty_weight, consts, own, *others, *donors)

    def sine_parts(halves):
        return call(
            functools.partial(sine_kernel, len(halves)),
            [shape((cells, width), bf16)] * len(halves),
            "sines",
            flops=12 * pairs,
            transcendentals=pairs,
            size=6 * pairs,
        )(*halves)

    study_penalty_weight, mean = lax.optimization_barrier((study_penalty_weight, mean))
    center, stride, beside = mean, 1, []
    for turn, radix in enumerate(digits(studies)):
        parts = swapped(center, stride, radix)
        stride *= radix
        if turn == 0:
            bases, sines = couplings(), sine_parts(halves[1:])
            beside = [*bases, *sines, *halves[:1]]
        elif turn == 1:
            sines = [*sine_parts(beside[-1:]), *beside[len(bases) : -1]]
            beside = [*beside[: len(bases)], *sines]
        center, *beside = lax.optimization_barrier((sum(parts, center), *beside))
    bases, sines = beside[: len(bases)], beside[len(bases) :]

    out, residual_freq = None, None
    part_shape = shape((depth, cells), f32)
    cost = dict(flops=2 * cells * width * depth, size=2 * cells * width)
    for block in range(1, blocks):
        base = bases[block : block + 1]
        if residual_freq is None:
            part, residual_freq = call(
                functools.partial(residual_kernel, block, window),
                [part_shape, shape((2 * depth, width), bf16)],
                "residual_part",
                **cost,
            )(consts, center, mean, freq_part, sines[block], *base)
        else:
            part = call(
                functools.partial(part_kernel, block, window), part_shape, "other_part", **cost
            )(consts, sines[block], residual_freq, *base)
        sent = rotated(part, blocks - block)
        out = sent if out is None else out + sent
    own_part = call(functools.partial(part_kernel, 0, window), part_shape, "own_part", **cost)(
        consts, sines[0], residual_freq, bases[0]
    )
    return jnp.swapaxes(own_part + out, 0, 1)[None]


def solution(mesh):
    in_specs = (P("study", "cell", None), P("study", "cell"), P("study"), P("study"), P(), P())
    out_specs = P("study", "cell", None)
    return jax.shard_map(
        on_device, mesh=mesh, in_specs=in_specs, out_specs=out_specs, check_vma=False
    )
```

```python
import functools
import math

import jax
import jax.numpy as jnp
from jax import lax
from jax.experimental import pallas as pl
from jax.experimental.pallas import tpu as pltpu
from jax.sharding import PartitionSpec as P

DONOR_LABELS = 16
FEATURE_PENALTY = 16.0
BLOCK = 1024
PAIR = 128
LANES = 128
PHASE_ROWS = 16
SUBLANES = 8
MIB = 1 << 20

COS_LEAD = -0.552051508388134
COS_TERMS = (-4.602194203577409, 9.359560663732573, -5.6907268683441155)
SIN_LEAD = 2.0 * COS_LEAD * abs(COS_LEAD)

VMEM_SPEC = pl.BlockSpec(memory_space=pltpu.VMEM)
SMEM_SPEC = pl.BlockSpec(memory_space=pltpu.SMEM)
HBM_SPEC = pl.BlockSpec(memory_space=pltpu.HBM)


def split3(x):
    hi = x.astype(jnp.bfloat16)
    rest = x - hi.astype(jnp.float32)
    mid = rest.astype(jnp.bfloat16)
    low = (rest - mid.astype(jnp.float32)).astype(jnp.bfloat16)
    return hi, mid, low


def block_start(block, cells):
    count = lax.axis_size("cell")
    return lax.rem(lax.axis_index("cell") + block, count) * cells


def valid_row(block, cells, length):
    position = lax.broadcasted_iota(jnp.int32, (1, cells), 1) + block_start(block, cells)
    return (position.astype(jnp.float32) < length).astype(jnp.float32)


def feature_scale(width):
    return math.sqrt(2.0 / (width * lax.axis_size("cell")))


def store_cells(x_ref, z, valid):
    depth, cells = z.shape
    z = (z.astype(jnp.float32) * valid).astype(jnp.bfloat16)
    for part in range(3):
        x_ref[part * depth : (part + 1) * depth, :] = z
    tail = x_ref.shape[0] - 3 * depth
    ones = jnp.where(lax.broadcasted_iota(jnp.int32, (tail, cells), 0) < 3, valid, 0.0)
    x_ref[3 * depth :, :] = ones.astype(jnp.bfloat16)


def setup_kernel(length_ref, freq_hbm, phase_hbm, z_hbm, w_ref, freq_ref, z_ref, x_ref, const_ref, phase_buf, sems):
    depth, width = freq_ref.shape
    start = pl.multiple_of(lax.axis_index("cell") * width, BLOCK)
    copies = [
        pltpu.make_async_copy(source, target, sems.at[i])
        for i, (source, target) in enumerate(
            [
                (z_hbm, z_ref),
                (phase_hbm.at[:, pl.ds(start, width)], phase_buf),
                (freq_hbm.at[:, pl.ds(start, width)], freq_ref),
            ]
        )
    ]
    for copy in copies:
        copy.start()
    length = jnp.full((1, 1), length_ref[0], jnp.int32).astype(jnp.float32)
    const_ref[...] = jnp.broadcast_to(length, const_ref.shape)
    row = 3 * depth + PHASE_ROWS
    w_ref[row:, :] = jnp.zeros((2 * PAIR - row, width), jnp.bfloat16)
    copies[0].wait()
    store_cells(x_ref, z_ref[...], valid_row(0, z_ref.shape[1], length))
    for copy in copies[1:]:
        copy.wait()
    turn = 1.0 / (2.0 * math.pi)
    for part, rows in enumerate(split3(freq_ref[...].astype(jnp.float32) * turn)):
        w_ref[part * depth : (part + 1) * depth, :] = rows
    hi, mid, low = [p.astype(jnp.float32) for p in split3(phase_buf[...] * turn)]
    index = lax.broadcasted_iota(jnp.int32, (PHASE_ROWS, width), 0)
    rows = jnp.where(index == 0, hi, jnp.where(index == 1, mid, jnp.where(index == 2, low, 0.0)))
    w_ref[3 * depth : row, :] = rows.astype(jnp.bfloat16)


def cosine_kernel(blocks, const_ref, w_ref, x_own_ref, *refs):
    z_refs = refs[: blocks - 1]
    s_refs = refs[blocks - 1 : 2 * blocks - 1]
    mean_ref = refs[2 * blocks - 1]
    x_refs = [x_own_ref, *refs[2 * blocks :]]
    width, cells = s_refs[0].shape
    length = const_ref[0:1, 0:1]
    for block in range(1, blocks):
        store_cells(x_refs[block], z_refs[block - 1][...], valid_row(block, cells, length))
    scale = feature_scale(width)
    per_length = 1.0 / length
    a, b, c = COS_TERMS
    strip = mean_ref.shape[1]
    for offset in range(0, width, BLOCK):
        here = slice(offset, offset + BLOCK)
        weights = w_ref[:, here].T
        squares = jnp.zeros((BLOCK, LANES), jnp.float32)
        for x_ref, s_ref in zip(x_refs, s_refs):
            t = jnp.dot(weights, x_ref[...], preferred_element_type=jnp.float32)
            r = t - jnp.round(t)
            u = r * r
            s = r * (((u + a) * u + b) * u + c)
            s_ref[here, :] = s
            for lane in range(0, cells, LANES):
                part = s[:, lane : lane + LANES]
                squares += part * part
        squares = jnp.sum(squares.T, axis=0, keepdims=True)
        mean = scale - (2.0 * scale * COS_LEAD * COS_LEAD) * per_length * squares
        for piece in range(0, BLOCK, LANES):
            row, column = divmod(offset + piece, strip)
            mean_ref[row : row + 1, column : column + LANES] = mean[:, piece : piece + LANES]


def sine_kernel(blocks, *refs):
    top = (1.0 + 2e-6) / (COS_LEAD * COS_LEAD)
    width = refs[0].shape[0]
    for s_ref, out_ref in zip(refs[:blocks], refs[blocks:]):
        for offset in range(0, width, BLOCK):
            here = slice(offset, offset + BLOCK)
            s = s_ref[here, :]
            rest = top - s * s
            out_ref[here, :] = (s * (rest * lax.rsqrt(rest))).astype(jnp.bfloat16)


def stacked(rows, cells):
    index = lax.broadcasted_iota(jnp.int32, (DONOR_LABELS, cells), 0)
    total = jnp.zeros((DONOR_LABELS, cells), jnp.float32)
    for k, row in enumerate(rows):
        if row is not None:
            total = jnp.where(index == k, row, total)
    return total.astype(jnp.bfloat16)


def coupling_kernel(blocks, owner, weight_ref, const_ref, *refs):
    z_refs, donor_refs, out_refs = refs[:blocks], refs[blocks : 2 * blocks], refs[2 * blocks :]
    depth, cells = out_refs[0].shape
    window = blocks * cells
    f32, bf16 = jnp.float32, jnp.bfloat16

    def compute():
        length = const_ref[0:1, 0:1]
        inverse_n = 1.0 / length
        label = lax.broadcasted_iota(jnp.int32, (DONOR_LABELS, cells), 0)
        members = [(ref[...] == label).astype(f32) for ref in donor_refs]
        valids = [valid_row(block, cells, length) for block in range(blocks)]
        counts = sum(
            jnp.sum(member * valid, axis=1, keepdims=True)
            for member, valid in zip(members, valids)
        )
        inverse = 1.0 / jnp.maximum(counts, 1.0)
        present = jnp.sum((counts > 0.5).astype(f32), axis=0, keepdims=True)
        one = jnp.ones((1, 1), f32)
        wides = [ref[...].astype(f32) for ref in z_refs]
        norms = [
            [p.astype(f32) for p in split3(-0.5 * jnp.sum(z * z, axis=0, keepdims=True))]
            for z in wides
        ]
        shares = [
            inverse_n * jnp.sum(member * inverse, axis=0, keepdims=True) for member in members
        ]
        same_zero = jnp.zeros((3 * DONOR_LABELS, cells), bf16)
        z_zero = jnp.zeros((depth, cells), bf16)
        rights = []
        for target in range(len(out_refs)):
            rest = [p.astype(f32) for p in split3(present * inverse_n * inverse_n - shares[target])]
            member = members[target].astype(bf16)
            exponent = [z_refs[target][...], stacked([one] * 3 + norms[target], cells), same_zero]
            pair = [z_zero, stacked([None] * 6 + [one] * 3 + rest, cells), member, member, member]
            rights.append(
                jnp.concatenate(
                    [jnp.concatenate(exponent, axis=0), jnp.concatenate(pair, axis=0)], axis=1
                )
            )
        totals = [jnp.zeros((PAIR, cells), f32) for _ in out_refs]
        for source in range(blocks):
            valid = valids[source]
            z = z_refs[source][...]
            minus = [p.astype(f32) for p in split3(-shares[source] * valid)]
            left = jnp.concatenate(
                [
                    z,
                    stacked(norms[source] + [one] * 3 + minus + [valid] * 3, cells),
                    *split3(members[source] * (inverse * inverse) * valid),
                ],
                axis=0,
            ).astype(f32).T.astype(bf16)
            rows = jnp.concatenate([z, jnp.ones((PAIR - depth, cells), bf16)], axis=0)
            for target, right in enumerate(rights):
                both = jnp.dot(left, right, preferred_element_type=f32)
                coupling = both[:, cells:] * jnp.exp2(both[:, :cells] * (math.log2(math.e) / depth))
                hi = coupling.astype(bf16)
                low = (coupling - hi.astype(f32)).astype(bf16)
                totals[target] += jnp.dot(rows, hi, preferred_element_type=f32)
                totals[target] += jnp.dot(rows, low, preferred_element_type=f32)
        scale = -(2.0 * window / depth) * jnp.full((1, 1), weight_ref[0], f32)
        for target, out_ref in enumerate(out_refs):
            total = totals[target]
            gradient = wides[target] * total[depth : depth + 1] - total[:depth]
            out_ref[...] = scale * valids[target] * gradient

    if owner is None:
        compute()
        return
    pl.when(lax.axis_index("cell") == owner)(compute)

    @pl.when(lax.axis_index("cell") != owner)
    def _():
        for out_ref in out_refs:
            out_ref[...] = jnp.zeros((depth, cells), f32)


def feature_part(block, const_ref, s_ref, rf_ref, window):
    width, cells = s_ref.shape
    depth = rf_ref.shape[0] // 2
    both = jnp.dot(rf_ref[...], s_ref[...], preferred_element_type=jnp.float32)
    length = const_ref[0:1, 0:1]
    factor = -(SIN_LEAD * window * feature_scale(width)) / length
    return factor * valid_row(block, cells, length) * (both[:depth] + both[depth:])


def residual_kernel(block, window, const_ref, sum_ref, mean_ref, freq_ref, s_ref, *refs):
    *base_refs, out_ref, rf_ref = refs
    strip = sum_ref.shape[1]
    depth = freq_ref.shape[0]
    center = sum_ref[...] * (1.0 / lax.axis_size("study"))
    residual = (2.0 * FEATURE_PENALTY) * (mean_ref[...] - center)
    for row in range(SUBLANES):
        here = slice(row * strip, (row + 1) * strip)
        rows = freq_ref[:, here].astype(jnp.float32) * residual[row : row + 1]
        hi = rows.astype(jnp.bfloat16)
        rf_ref[:depth, here] = hi
        rf_ref[depth:, here] = (rows - hi.astype(jnp.float32)).astype(jnp.bfloat16)
    part_kernel(block, window, const_ref, s_ref, rf_ref, *base_refs, out_ref)


def part_kernel(block, window, const_ref, s_ref, rf_ref, *refs):
    *base_refs, out_ref = refs
    part = feature_part(block, const_ref, s_ref, rf_ref, window)
    out_ref[...] = sum((ref[...] for ref in base_refs), part)


def call(kernel, out_shape, name, flops, transcendentals=0, size=0, scratch=(), vmem=8, in_specs=None):
    several = isinstance(out_shape, (list, tuple))

    def run(*operands):
        return pl.pallas_call(
            kernel,
            out_shape=out_shape,
            in_specs=in_specs or [VMEM_SPEC] * len(operands),
            out_specs=[VMEM_SPEC] * len(out_shape) if several else VMEM_SPEC,
            scratch_shapes=list(scratch),
            compiler_params=pltpu.CompilerParams(vmem_limit_bytes=vmem * MIB),
            cost_estimate=pl.CostEstimate(
                flops=int(flops), bytes_accessed=int(size), transcendentals=int(transcendentals)
            ),
            name=name,
        )(*operands)

    return run


def in_hbm(x):
    return pltpu.with_memory_space_constraint(x, pltpu.HBM)


def rotated(x, shift):
    count = lax.axis_size("cell")
    return lax.ppermute(x, "cell", [((i + shift) % count, i) for i in range(count)])


def digits(count):
    radices = []
    while count > 1:
        radix = next(r for r in (4, 2, *range(3, count + 1)) if count % r == 0)
        radices.append(radix)
        count //= radix
    return radices


def swapped(x, stride, radix):
    count = lax.axis_size("study")

    def partner(i, k):
        digit = i // stride % radix
        other = digit ^ k if radix & (radix - 1) == 0 else (digit + k) % radix
        return i + (other - digit) * stride

    return [
        lax.ppermute(x, "study", [(i, partner(i, k)) for i in range(count)])
        for k in range(radix - 1, 0, -1)
    ]


def on_device(latents, donor_ids, study_valid_length, study_penalty_weight, frequencies, phases):
    own = jnp.swapaxes(latents[0], 0, 1)
    depth, cells = own.shape
    blocks = lax.axis_size("cell")
    studies = lax.axis_size("study")
    features = frequencies.shape[1]
    width = features // blocks
    window = blocks * cells
    strip = width // SUBLANES
    f32, bf16 = jnp.float32, jnp.bfloat16
    shape = jax.ShapeDtypeStruct
    pairs = window * width

    others = [rotated(own, k) for k in range(1, blocks)]
    donors = [donor_ids] + [rotated(donor_ids, k) for k in range(1, blocks)]

    turn_weights, freq_part, own, x_own, consts = call(
        setup_kernel,
        [
            shape((2 * PAIR, width), bf16),
            shape((depth, width), bf16),
            shape((depth, cells), bf16),
            shape((2 * PAIR, cells), bf16),
            shape((1, 128), f32),
        ],
        "setup",
        flops=20 * depth * width,
        size=4 * depth * width,
        scratch=[pltpu.VMEM((1, width), f32), pltpu.SemaphoreType.DMA((3,))],
        in_specs=[SMEM_SPEC] + [HBM_SPEC] * 3,
    )(
        study_valid_length,
        *[in_hbm(x) for x in (frequencies, phases.reshape(1, features), own)],
    )

    *halves, mean = call(
        functools.partial(cosine_kernel, blocks),
        [shape((width, cells), f32)] * blocks + [shape((SUBLANES, strip), f32)],
        "cosine_sums",
        flops=4 * PAIR * pairs + 12 * pairs,
        size=4 * PAIR * width,
        scratch=[pltpu.VMEM((2 * PAIR, cells), bf16)] * (blocks - 1),
    )(consts, turn_weights, x_own, *others)

    def couplings():
        outputs, owner = (2, 1) if blocks == 2 else (1, None)
        return call(
            functools.partial(coupling_kernel, blocks, owner),
            [shape((depth, cells), f32)] * outputs,
            "coupling",
            flops=2 * cells * window * (3 * depth),
            transcendentals=cells * window,
            size=4 * cells * depth,
            in_specs=[SMEM_SPEC] + [VMEM_SPEC] * (1 + 2 * blocks),
        )(study_penalty_weight, consts, own, *others, *donors)

    def sine_parts(halves):
        return call(
            functools.partial(sine_kernel, len(halves)),
            [shape((width, cells), bf16)] * len(halves),
            "sines",
            flops=12 * pairs,
            transcendentals=pairs,
            size=6 * pairs,
        )(*halves)

    study_penalty_weight, mean = lax.optimization_barrier((study_penalty_weight, mean))
    center, stride, beside = mean, 1, []
    for turn, radix in enumerate(digits(studies)):
        parts = swapped(center, stride, radix)
        stride *= radix
        if turn == 0:
            bases, sines = couplings(), sine_parts(halves[1:])
            beside = [*bases, *sines, *halves[:1]]
        elif turn == 1:
            sines = [*sine_parts(beside[-1:]), *beside[len(bases) : -1]]
            beside = [*beside[: len(bases)], *sines]
        center, *beside = lax.optimization_barrier((sum(parts, center), *beside))
    bases, sines = beside[: len(bases)], beside[len(bases) :]

    out, residual_freq = None, None
    part_shape = shape((depth, cells), f32)
    cost = dict(flops=2 * cells * width * depth, size=2 * cells * width)
    for block in range(1, blocks):
        base = bases[block : block + 1]
        if residual_freq is None:
            part, residual_freq = call(
                functools.partial(residual_kernel, block, window),
                [part_shape, shape((2 * depth, width), bf16)],
                "residual_part",
                **cost,
            )(consts, center, mean, freq_part, sines[block], *base)
        else:
            part = call(
                functools.partial(part_kernel, block, window), part_shape, "other_part", **cost
            )(consts, sines[block], residual_freq, *base)
        sent = rotated(part, blocks - block)
        out = sent if out is None else out + sent
    own_part = call(functools.partial(part_kernel, 0, window), part_shape, "own_part", **cost)(
        consts, sines[0], residual_freq, bases[0]
    )
    return jnp.swapaxes(own_part + out, 0, 1)[None]


def solution(mesh):
    in_specs = (P("study", "cell", None), P("study", "cell"), P("study"), P("study"), P(), P())
    out_specs = P("study", "cell", None)
    return jax.shard_map(
        on_device, mesh=mesh, in_specs=in_specs, out_specs=out_specs, check_vma=False
    )
```

```python
import functools
import math

import jax
import jax.numpy as jnp
from jax import lax
from jax.experimental import pallas as pl
from jax.experimental.pallas import tpu as pltpu
from jax.sharding import PartitionSpec as P

DONOR_LABELS = 16
FEATURE_PENALTY = 16.0
BLOCK = 1024
PAIR = 128
LANES = 128
PHASE_ROWS = 16
SUBLANES = 8
MIB = 1 << 20

COS_LEAD = -0.552051508388134
COS_TERMS = (-4.602194203577409, 9.359560663732573, -5.6907268683441155)
SIN_LEAD = 2.0 * COS_LEAD * abs(COS_LEAD)

VMEM_SPEC = pl.BlockSpec(memory_space=pltpu.VMEM)
SMEM_SPEC = pl.BlockSpec(memory_space=pltpu.SMEM)
HBM_SPEC = pl.BlockSpec(memory_space=pltpu.HBM)


def split3(x):
    hi = x.astype(jnp.bfloat16)
    rest = x - hi.astype(jnp.float32)
    mid = rest.astype(jnp.bfloat16)
    low = (rest - mid.astype(jnp.float32)).astype(jnp.bfloat16)
    return hi, mid, low


def block_start(block, cells):
    count = lax.axis_size("cell")
    return lax.rem(lax.axis_index("cell") + block, count) * cells


def valid_row(block, cells, length):
    position = lax.broadcasted_iota(jnp.int32, (1, cells), 1) + block_start(block, cells)
    return (position.astype(jnp.float32) < length).astype(jnp.float32)


def feature_scale(width):
    return math.sqrt(2.0 / (width * lax.axis_size("cell")))


def store_cells(x_ref, z, valid):
    depth, cells = z.shape
    z = (z.astype(jnp.float32) * valid).astype(jnp.bfloat16)
    for part in range(3):
        x_ref[part * depth : (part + 1) * depth, :] = z
    tail = x_ref.shape[0] - 3 * depth
    ones = jnp.where(lax.broadcasted_iota(jnp.int32, (tail, cells), 0) < 3, valid, 0.0)
    x_ref[3 * depth :, :] = ones.astype(jnp.bfloat16)


def setup_kernel(length_ref, freq_hbm, phase_hbm, z_hbm, w_ref, freq_ref, z_ref, x_ref, const_ref, phase_buf, sems):
    depth, width = freq_ref.shape
    start = pl.multiple_of(lax.axis_index("cell") * width, BLOCK)
    copies = [
        pltpu.make_async_copy(source, target, sems.at[i])
        for i, (source, target) in enumerate(
            [
                (z_hbm, z_ref),
                (phase_hbm.at[:, pl.ds(start, width)], phase_buf),
                (freq_hbm.at[:, pl.ds(start, width)], freq_ref),
            ]
        )
    ]
    for copy in copies:
        copy.start()
    length = jnp.full((1, 1), length_ref[0], jnp.int32).astype(jnp.float32)
    const_ref[...] = jnp.broadcast_to(length, const_ref.shape)
    row = 3 * depth + PHASE_ROWS
    w_ref[row:, :] = jnp.zeros((2 * PAIR - row, width), jnp.bfloat16)
    copies[0].wait()
    store_cells(x_ref, z_ref[...], valid_row(0, z_ref.shape[1], length))
    for copy in copies[1:]:
        copy.wait()
    turn = 1.0 / (2.0 * math.pi)
    for part, rows in enumerate(split3(freq_ref[...].astype(jnp.float32) * turn)):
        w_ref[part * depth : (part + 1) * depth, :] = rows
    hi, mid, low = [p.astype(jnp.float32) for p in split3(phase_buf[...] * turn)]
    index = lax.broadcasted_iota(jnp.int32, (PHASE_ROWS, width), 0)
    rows = jnp.where(index == 0, hi, jnp.where(index == 1, mid, jnp.where(index == 2, low, 0.0)))
    w_ref[3 * depth : row, :] = rows.astype(jnp.bfloat16)


def cosine_kernel(blocks, const_ref, w_ref, x_own_ref, *refs):
    z_refs = refs[: blocks - 1]
    s_refs = refs[blocks - 1 : 2 * blocks - 1]
    mean_ref = refs[2 * blocks - 1]
    x_refs = [x_own_ref, *refs[2 * blocks :]]
    width, cells = s_refs[0].shape
    length = const_ref[0:1, 0:1]
    for block in range(1, blocks):
        store_cells(x_refs[block], z_refs[block - 1][...], valid_row(block, cells, length))
    scale = feature_scale(width)
    per_length = 1.0 / length
    a, b, c = COS_TERMS
    strip = mean_ref.shape[1]
    for offset in range(0, width, BLOCK):
        here = slice(offset, offset + BLOCK)
        weights = w_ref[:, here].T
        squares = jnp.zeros((BLOCK, LANES), jnp.float32)
        for x_ref, s_ref in zip(x_refs, s_refs):
            t = jnp.dot(weights, x_ref[...], preferred_element_type=jnp.float32)
            r = t - jnp.round(t)
            u = r * r
            s = r * (((u + a) * u + b) * u + c)
            s_ref[here, :] = s
            for lane in range(0, cells, LANES):
                part = s[:, lane : lane + LANES]
                squares += part * part
        squares = jnp.sum(squares.T, axis=0, keepdims=True)
        mean = scale - (2.0 * scale * COS_LEAD * COS_LEAD) * per_length * squares
        for piece in range(0, BLOCK, LANES):
            row, column = divmod(offset + piece, strip)
            mean_ref[row : row + 1, column : column + LANES] = mean[:, piece : piece + LANES]


def sine_kernel(blocks, *refs):
    top = (1.0 + 2e-6) / (COS_LEAD * COS_LEAD)
    width = refs[0].shape[0]
    for s_ref, out_ref in zip(refs[:blocks], refs[blocks:]):
        for offset in range(0, width, BLOCK):
            here = slice(offset, offset + BLOCK)
            s = s_ref[here, :]
            rest = top - s * s
            out_ref[here, :] = (s * (rest * lax.rsqrt(rest))).astype(jnp.bfloat16)


def stacked(rows, cells):
    index = lax.broadcasted_iota(jnp.int32, (DONOR_LABELS, cells), 0)
    total = jnp.zeros((DONOR_LABELS, cells), jnp.float32)
    for k, row in enumerate(rows):
        if row is not None:
            total = jnp.where(index == k, row, total)
    return total.astype(jnp.bfloat16)


def coupling_kernel(blocks, owner, weight_ref, const_ref, *refs):
    z_refs, donor_refs, out_refs = refs[:blocks], refs[blocks : 2 * blocks], refs[2 * blocks :]
    depth, cells = out_refs[0].shape
    window = blocks * cells
    f32, bf16 = jnp.float32, jnp.bfloat16

    def compute():
        length = const_ref[0:1, 0:1]
        inverse_n = 1.0 / length
        label = lax.broadcasted_iota(jnp.int32, (DONOR_LABELS, cells), 0)
        members = [(ref[...] == label).astype(f32) for ref in donor_refs]
        valids = [valid_row(block, cells, length) for block in range(blocks)]
        counts = sum(
            jnp.sum(member * valid, axis=1, keepdims=True)
            for member, valid in zip(members, valids)
        )
        inverse = 1.0 / jnp.maximum(counts, 1.0)
        present = jnp.sum((counts > 0.5).astype(f32), axis=0, keepdims=True)
        one = jnp.ones((1, 1), f32)
        wides = [ref[...].astype(f32) for ref in z_refs]
        norms = [
            [p.astype(f32) for p in split3(-0.5 * jnp.sum(z * z, axis=0, keepdims=True))]
            for z in wides
        ]
        shares = [
            inverse_n * jnp.sum(member * inverse, axis=0, keepdims=True) for member in members
        ]
        same_zero = jnp.zeros((3 * DONOR_LABELS, cells), bf16)
        z_zero = jnp.zeros((depth, cells), bf16)
        rights = []
        for target in range(len(out_refs)):
            rest = [p.astype(f32) for p in split3(present * inverse_n * inverse_n - shares[target])]
            member = members[target].astype(bf16)
            exponent = [z_refs[target][...], stacked([one] * 3 + norms[target], cells), same_zero]
            pair = [z_zero, stacked([None] * 6 + [one] * 3 + rest, cells), member, member, member]
            rights.append(
                jnp.concatenate(
                    [jnp.concatenate(exponent, axis=0), jnp.concatenate(pair, axis=0)], axis=1
                )
            )
        totals = [jnp.zeros((PAIR, cells), f32) for _ in out_refs]
        for source in range(blocks):
            valid = valids[source]
            z = z_refs[source][...]
            minus = [p.astype(f32) for p in split3(-shares[source] * valid)]
            left = jnp.concatenate(
                [
                    z,
                    stacked(norms[source] + [one] * 3 + minus + [valid] * 3, cells),
                    *split3(members[source] * (inverse * inverse) * valid),
                ],
                axis=0,
            ).astype(f32).T.astype(bf16)
            rows = jnp.concatenate([z, jnp.ones((PAIR - depth, cells), bf16)], axis=0)
            for target, right in enumerate(rights):
                both = jnp.dot(left, right, preferred_element_type=f32)
                coupling = both[:, cells:] * jnp.exp2(both[:, :cells] * (math.log2(math.e) / depth))
                hi = coupling.astype(bf16)
                low = (coupling - hi.astype(f32)).astype(bf16)
                totals[target] += jnp.dot(rows, hi, preferred_element_type=f32)
                totals[target] += jnp.dot(rows, low, preferred_element_type=f32)
        scale = -(2.0 * window / depth) * jnp.full((1, 1), weight_ref[0], f32)
        for target, out_ref in enumerate(out_refs):
            total = totals[target]
            gradient = wides[target] * total[depth : depth + 1] - total[:depth]
            out_ref[...] = scale * valids[target] * gradient

    if owner is None:
        compute()
        return
    pl.when(lax.axis_index("cell") == owner)(compute)

    @pl.when(lax.axis_index("cell") != owner)
    def _():
        for out_ref in out_refs:
            out_ref[...] = jnp.zeros((depth, cells), f32)


def feature_part(block, const_ref, s_ref, rf_ref, window):
    width, cells = s_ref.shape
    depth = rf_ref.shape[0] // 2
    both = jnp.dot(rf_ref[...], s_ref[...], preferred_element_type=jnp.float32)
    length = const_ref[0:1, 0:1]
    factor = -(SIN_LEAD * window * feature_scale(width)) / length
    return factor * valid_row(block, cells, length) * (both[:depth] + both[depth:])


def residual_kernel(block, window, const_ref, sum_ref, mean_ref, freq_ref, s_ref, *refs):
    *base_refs, out_ref, rf_ref = refs
    strip = sum_ref.shape[1]
    depth = freq_ref.shape[0]
    center = sum_ref[...] * (1.0 / lax.axis_size("study"))
    residual = (2.0 * FEATURE_PENALTY) * (mean_ref[...] - center)
    for row in range(SUBLANES):
        here = slice(row * strip, (row + 1) * strip)
        rows = freq_ref[:, here].astype(jnp.float32) * residual[row : row + 1]
        hi = rows.astype(jnp.bfloat16)
        rf_ref[:depth, here] = hi
        rf_ref[depth:, here] = (rows - hi.astype(jnp.float32)).astype(jnp.bfloat16)
    part_kernel(block, window, const_ref, s_ref, rf_ref, *base_refs, out_ref)


def part_kernel(block, window, const_ref, s_ref, rf_ref, *refs):
    *base_refs, out_ref = refs
    part = feature_part(block, const_ref, s_ref, rf_ref, window)
    out_ref[...] = sum((ref[...] for ref in base_refs), part)


def call(kernel, out_shape, name, flops, transcendentals=0, size=0, scratch=(), vmem=8, in_specs=None):
    several = isinstance(out_shape, (list, tuple))

    def run(*operands):
        return pl.pallas_call(
            kernel,
            out_shape=out_shape,
            in_specs=in_specs or [VMEM_SPEC] * len(operands),
            out_specs=[VMEM_SPEC] * len(out_shape) if several else VMEM_SPEC,
            scratch_shapes=list(scratch),
            compiler_params=pltpu.CompilerParams(vmem_limit_bytes=vmem * MIB),
            cost_estimate=pl.CostEstimate(
                flops=int(flops), bytes_accessed=int(size), transcendentals=int(transcendentals)
            ),
            name=name,
        )(*operands)

    return run


def in_hbm(x):
    return pltpu.with_memory_space_constraint(x, pltpu.HBM)


def rotated(x, shift):
    count = lax.axis_size("cell")
    return lax.ppermute(x, "cell", [((i + shift) % count, i) for i in range(count)])


def rounds(count):
    stride = 1
    while stride < count:
        left = count // stride
        radix = 4 if stride == 1 and left % 4 == 0 else next(r for r in range(2, left + 1) if left % r == 0)
        yield stride, radix
        stride *= radix


def swapped(x, stride, radix):
    count = lax.axis_size("study")

    def partner(i, k):
        digit = i // stride % radix
        other = digit ^ k if radix & (radix - 1) == 0 else (digit + k) % radix
        return i + (other - digit) * stride

    return [
        lax.ppermute(x, "study", [(i, partner(i, k)) for i in range(count)])
        for k in range(radix - 1, 0, -1)
    ]


def on_device(latents, donor_ids, study_valid_length, study_penalty_weight, frequencies, phases):
    own = jnp.swapaxes(latents[0], 0, 1)
    depth, cells = own.shape
    blocks = lax.axis_size("cell")
    studies = lax.axis_size("study")
    features = frequencies.shape[1]
    width = features // blocks
    window = blocks * cells
    strip = width // SUBLANES
    f32, bf16 = jnp.float32, jnp.bfloat16
    shape = jax.ShapeDtypeStruct
    pairs = window * width

    others = [rotated(own, k) for k in range(1, blocks)]
    donors = [donor_ids] + [rotated(donor_ids, k) for k in range(1, blocks)]

    turn_weights, freq_part, own, x_own, consts = call(
        setup_kernel,
        [
            shape((2 * PAIR, width), bf16),
            shape((depth, width), bf16),
            shape((depth, cells), bf16),
            shape((2 * PAIR, cells), bf16),
            shape((1, 128), f32),
        ],
        "setup",
        flops=20 * depth * width,
        size=4 * depth * width,
        scratch=[pltpu.VMEM((1, width), f32), pltpu.SemaphoreType.DMA((3,))],
        in_specs=[SMEM_SPEC] + [HBM_SPEC] * 3,
    )(
        study_valid_length,
        *[in_hbm(x) for x in (frequencies, phases.reshape(1, features), own)],
    )

    *halves, mean = call(
        functools.partial(cosine_kernel, blocks),
        [shape((width, cells), f32)] * blocks + [shape((SUBLANES, strip), f32)],
        "cosine_sums",
        flops=4 * PAIR * pairs + 12 * pairs,
        size=4 * PAIR * width,
        scratch=[pltpu.VMEM((2 * PAIR, cells), bf16)] * (blocks - 1),
    )(consts, turn_weights, x_own, *others)

    def couplings():
        outputs, owner = (2, 1) if blocks == 2 else (1, None)
        return call(
            functools.partial(coupling_kernel, blocks, owner),
            [shape((depth, cells), f32)] * outputs,
            "coupling",
            flops=2 * cells * window * (3 * depth),
            transcendentals=cells * window,
            size=4 * cells * depth,
            in_specs=[SMEM_SPEC] + [VMEM_SPEC] * (1 + 2 * blocks),
        )(study_penalty_weight, consts, own, *others, *donors)

    def sine_parts(halves):
        return call(
            functools.partial(sine_kernel, len(halves)),
            [shape((width, cells), bf16)] * len(halves),
            "sines",
            flops=12 * pairs,
            transcendentals=pairs,
            size=6 * pairs,
        )(*halves)

    study_penalty_weight, mean = lax.optimization_barrier((study_penalty_weight, mean))
    center, own_half, done = mean, halves[0], []
    steps = [lambda: sine_parts(halves[1:]), couplings, lambda: sine_parts([own_half])]
    for stride, radix in rounds(studies):
        parts = swapped(center, stride, radix)
        made = steps[len(done)]() if len(done) < len(steps) else []
        later = [own_half] if len(done) < len(steps) - 1 else []
        center, *made = lax.optimization_barrier((sum(parts, center), *made, *later))
        if later:
            own_half = made.pop()
        if len(done) < len(steps):
            done.append(made)
    while len(done) < len(steps):
        done.append(steps[len(done)]())
    sines, bases = [*done[2], *done[0]], done[1]

    out, residual_freq = None, None
    part_shape = shape((depth, cells), f32)
    cost = dict(flops=2 * cells * width * depth, size=2 * cells * width)
    for block in range(1, blocks):
        base = bases[block : block + 1]
        if residual_freq is None:
            part, residual_freq = call(
                functools.partial(residual_kernel, block, window),
                [part_shape, shape((2 * depth, width), bf16)],
                "residual_part",
                **cost,
            )(consts, center, mean, freq_part, sines[block], *base)
        else:
            part = call(
                functools.partial(part_kernel, block, window), part_shape, "other_part", **cost
            )(consts, sines[block], residual_freq, *base)
        sent = rotated(part, blocks - block)
        out = sent if out is None else out + sent
    own_part = call(functools.partial(part_kernel, 0, window), part_shape, "own_part", **cost)(
        consts, sines[0], residual_freq, bases[0]
    )
    return jnp.swapaxes(own_part + out, 0, 1)[None]


def solution(mesh):
    in_specs = (P("study", "cell", None), P("study", "cell"), P("study"), P("study"), P(), P())
    out_specs = P("study", "cell", None)
    return jax.shard_map(
        on_device, mesh=mesh, in_specs=in_specs, out_specs=out_specs, check_vma=False
    )
```

```python
import functools
import math
from typing import NamedTuple

import jax
import jax.numpy as jnp
from jax import lax
from jax.experimental import pallas as pl
from jax.experimental.pallas import tpu as pltpu
from jax.sharding import PartitionSpec as P

DONOR_LABELS = 16
FEATURE_PENALTY = 16.0
BLOCK = 1024
PAIR = 128
WIDE_CORE = 1
SHIFT = 4
LANES = 128
PHASE_ROWS = 16
SUBLANES = 8
MIB = 1 << 20

COS_LEAD = -0.552051508388134
COS_TERMS = (-4.602194203577409, 9.359560663732573, -5.6907268683441155)
SIN_LEAD = 2.0 * COS_LEAD * abs(COS_LEAD)

VMEM_SPEC = pl.BlockSpec(memory_space=pltpu.VMEM)
SMEM_SPEC = pl.BlockSpec(memory_space=pltpu.SMEM)
HBM_SPEC = pl.BlockSpec(memory_space=pltpu.HBM)


def split3(x):
    hi = x.astype(jnp.bfloat16)
    rest = x - hi.astype(jnp.float32)
    mid = rest.astype(jnp.bfloat16)
    low = (rest - mid.astype(jnp.float32)).astype(jnp.bfloat16)
    return hi, mid, low


def block_start(block, cells):
    count = lax.axis_size("cell")
    return lax.rem(lax.axis_index("cell") + block, count) * cells


def valid_row(block, cells, length):
    position = lax.broadcasted_iota(jnp.int32, (1, cells), 1) + block_start(block, cells)
    return (position.astype(jnp.float32) < length).astype(jnp.float32)


class Split(NamedTuple):
    features: int
    narrow: int
    wide: int

    @property
    def scale(self):
        return math.sqrt(2.0 / self.features)

    @property
    def rows(self):
        return next(r for r in range(SUBLANES, 0, -1) if self.wide % (r * LANES) == 0)

    def start(self):
        return pl.multiple_of(lax.axis_index("cell") * self.narrow, LANES)

    def extra(self, body):
        if self.wide > self.narrow:
            pl.when(lax.axis_index("cell") == WIDE_CORE)(body)

    def over_blocks(self, body):
        def over(start, stop):
            for offset in range(start, stop, BLOCK):
                body(offset, min(BLOCK, stop - offset))

        over(0, self.narrow)
        self.extra(lambda: over(self.narrow, self.wide))


def split_features(features, blocks):
    even = features // blocks
    shift = even * SHIFT // (LANES * 32) * LANES if blocks == 2 else 0
    return Split(features, even - shift, even + shift)


def store_cells(x_ref, z, valid):
    depth, cells = z.shape
    z = (z.astype(jnp.float32) * valid).astype(jnp.bfloat16)
    for part in range(3):
        x_ref[part * depth : (part + 1) * depth, :] = z
    tail = x_ref.shape[0] - 3 * depth
    ones = jnp.where(lax.broadcasted_iota(jnp.int32, (tail, cells), 0) < 3, valid, 0.0)
    x_ref[3 * depth :, :] = ones.astype(jnp.bfloat16)


def setup_kernel(split, length_ref, freq_hbm, phase_hbm, z_hbm, w_ref, freq_ref, z_ref, x_ref, const_ref, phase_buf, sems):
    depth, width = freq_ref.shape
    start = split.start()
    copies = [
        pltpu.make_async_copy(source, target, sems.at[i])
        for i, (source, target) in enumerate(
            [
                (z_hbm, z_ref),
                (phase_hbm.at[:, pl.ds(start, width)], phase_buf),
                (freq_hbm.at[:, pl.ds(start, width)], freq_ref),
            ]
        )
    ]
    for copy in copies:
        copy.start()
    length = jnp.full((1, 1), length_ref[0], jnp.int32).astype(jnp.float32)
    const_ref[...] = jnp.broadcast_to(length, const_ref.shape)
    row = 3 * depth + PHASE_ROWS
    w_ref[row:, :] = jnp.zeros((2 * PAIR - row, width), jnp.bfloat16)
    copies[0].wait()
    store_cells(x_ref, z_ref[...], valid_row(0, z_ref.shape[1], length))
    for copy in copies[1:]:
        copy.wait()
    turn = 1.0 / (2.0 * math.pi)
    for part, rows in enumerate(split3(freq_ref[...].astype(jnp.float32) * turn)):
        w_ref[part * depth : (part + 1) * depth, :] = rows
    hi, mid, low = [p.astype(jnp.float32) for p in split3(phase_buf[...] * turn)]
    index = lax.broadcasted_iota(jnp.int32, (PHASE_ROWS, width), 0)
    rows = jnp.where(index == 0, hi, jnp.where(index == 1, mid, jnp.where(index == 2, low, 0.0)))
    w_ref[3 * depth : row, :] = rows.astype(jnp.bfloat16)


def cosine_kernel(split, blocks, const_ref, w_ref, x_own_ref, *refs):
    z_refs = refs[: blocks - 1]
    s_refs = refs[blocks - 1 : 2 * blocks - 1]
    mean_ref = refs[2 * blocks - 1]
    x_refs = [x_own_ref, *refs[2 * blocks :]]
    width, cells = s_refs[0].shape
    length = const_ref[0:1, 0:1]
    for block in range(1, blocks):
        store_cells(x_refs[block], z_refs[block - 1][...], valid_row(block, cells, length))
    scale = split.scale
    per_length = 1.0 / length
    a, b, c = COS_TERMS
    strip = mean_ref.shape[1]
    mean_ref[...] = jnp.zeros_like(mean_ref)

    def one_block(offset, size):
        here = slice(offset, offset + size)
        weights = w_ref[:, here].T
        squares = jnp.zeros((size, LANES), jnp.float32)
        for x_ref, s_ref in zip(x_refs, s_refs):
            t = jnp.dot(weights, x_ref[...], preferred_element_type=jnp.float32)
            r = t - jnp.round(t)
            u = r * r
            s = r * (((u + a) * u + b) * u + c)
            s_ref[here, :] = s
            for lane in range(0, cells, LANES):
                part = s[:, lane : lane + LANES]
                squares += part * part
        squares = jnp.sum(squares.T, axis=0, keepdims=True)
        mean = scale - (2.0 * scale * COS_LEAD * COS_LEAD) * per_length * squares
        for piece in range(0, size, LANES):
            row, column = divmod(offset + piece, strip)
            mean_ref[row : row + 1, column : column + LANES] = mean[:, piece : piece + LANES]

    split.over_blocks(one_block)


def sine_kernel(split, blocks, *refs):
    top = (1.0 + 2e-6) / (COS_LEAD * COS_LEAD)

    def one_block(offset, size):
        here = slice(offset, offset + size)
        for s_ref, out_ref in zip(refs[:blocks], refs[blocks:]):
            s = s_ref[here, :]
            rest = top - s * s
            out_ref[here, :] = (s * (rest * lax.rsqrt(rest))).astype(jnp.bfloat16)

    split.over_blocks(one_block)


def stacked(rows, cells):
    index = lax.broadcasted_iota(jnp.int32, (DONOR_LABELS, cells), 0)
    total = jnp.zeros((DONOR_LABELS, cells), jnp.float32)
    for k, row in enumerate(rows):
        if row is not None:
            total = jnp.where(index == k, row, total)
    return total.astype(jnp.bfloat16)


def coupling_kernel(blocks, weight_ref, const_ref, *refs):
    z_refs, donor_refs, out_refs = refs[:blocks], refs[blocks : 2 * blocks], refs[2 * blocks :]
    depth, cells = out_refs[0].shape
    window = blocks * cells
    f32, bf16 = jnp.float32, jnp.bfloat16
    length = const_ref[0:1, 0:1]
    inverse_n = 1.0 / length
    label = lax.broadcasted_iota(jnp.int32, (DONOR_LABELS, cells), 0)
    members = [(ref[...] == label).astype(f32) for ref in donor_refs]
    valids = [valid_row(block, cells, length) for block in range(blocks)]
    counts = sum(
        jnp.sum(member * valid, axis=1, keepdims=True)
        for member, valid in zip(members, valids)
    )
    inverse = 1.0 / jnp.maximum(counts, 1.0)
    present = jnp.sum((counts > 0.5).astype(f32), axis=0, keepdims=True)
    one = jnp.ones((1, 1), f32)
    wides = [ref[...].astype(f32) for ref in z_refs]
    norms = [
        [p.astype(f32) for p in split3(-0.5 * jnp.sum(z * z, axis=0, keepdims=True))]
        for z in wides
    ]
    shares = [
        inverse_n * jnp.sum(member * inverse, axis=0, keepdims=True) for member in members
    ]
    same_zero = jnp.zeros((3 * DONOR_LABELS, cells), bf16)
    z_zero = jnp.zeros((depth, cells), bf16)
    rights = []
    for target in range(len(out_refs)):
        rest = [p.astype(f32) for p in split3(present * inverse_n * inverse_n - shares[target])]
        member = members[target].astype(bf16)
        exponent = [z_refs[target][...], stacked([one] * 3 + norms[target], cells), same_zero]
        pair = [z_zero, stacked([None] * 6 + [one] * 3 + rest, cells), member, member, member]
        rights.append(
            jnp.concatenate(
                [jnp.concatenate(exponent, axis=0), jnp.concatenate(pair, axis=0)], axis=1
            )
        )
    totals = [jnp.zeros((PAIR, cells), f32) for _ in out_refs]
    for source in range(blocks):
        valid = valids[source]
        z = z_refs[source][...]
        minus = [p.astype(f32) for p in split3(-shares[source] * valid)]
        left = jnp.concatenate(
            [
                z,
                stacked(norms[source] + [one] * 3 + minus + [valid] * 3, cells),
                *split3(members[source] * (inverse * inverse) * valid),
            ],
            axis=0,
        ).astype(f32).T.astype(bf16)
        rows = jnp.concatenate([z, jnp.ones((PAIR - depth, cells), bf16)], axis=0)
        for target, right in enumerate(rights):
            both = jnp.dot(left, right, preferred_element_type=f32)
            coupling = both[:, cells:] * jnp.exp2(both[:, :cells] * (math.log2(math.e) / depth))
            hi = coupling.astype(bf16)
            low = (coupling - hi.astype(f32)).astype(bf16)
            totals[target] += jnp.dot(rows, hi, preferred_element_type=f32)
            totals[target] += jnp.dot(rows, low, preferred_element_type=f32)
    scale = -(2.0 * window / depth) * jnp.full((1, 1), weight_ref[0], f32)
    for target, out_ref in enumerate(out_refs):
        total = totals[target]
        gradient = wides[target] * total[depth : depth + 1] - total[:depth]
        out_ref[...] = scale * valids[target] * gradient


def residual_kernel(split, block, window, const_ref, sum_ref, mean_ref, freq_ref, s_ref, *refs):
    *base_refs, out_ref, rf_ref = refs
    rows, strip = sum_ref.shape
    depth = freq_ref.shape[0]
    center = sum_ref[...] * (1.0 / lax.axis_size("study"))
    residual = (2.0 * FEATURE_PENALTY) * (mean_ref[...] - center)
    for row in range(rows):
        here = slice(row * strip, (row + 1) * strip)
        product = freq_ref[:, here].astype(jnp.float32) * residual[row : row + 1]
        hi = product.astype(jnp.bfloat16)
        rf_ref[:depth, here] = hi
        rf_ref[depth:, here] = (product - hi.astype(jnp.float32)).astype(jnp.bfloat16)
    part_kernel(split, block, window, const_ref, s_ref, rf_ref, *base_refs, out_ref)


def part_kernel(split, block, window, const_ref, s_ref, rf_ref, *refs):
    *base_refs, out_ref = refs
    depth, cells = out_ref.shape
    length = const_ref[0:1, 0:1]
    factor = -(SIN_LEAD * window * split.scale) / length * valid_row(block, cells, length)

    def part(here):
        both = jnp.dot(rf_ref[:, here], s_ref[here, :], preferred_element_type=jnp.float32)
        return factor * (both[:depth] + both[depth:])

    out_ref[...] = sum((ref[...] for ref in base_refs), part(slice(0, split.narrow)))

    def add_extra():
        out_ref[...] += part(slice(split.narrow, split.wide))

    split.extra(add_extra)


def call(kernel, out_shape, name, flops, transcendentals=0, size=0, scratch=(), vmem=8, in_specs=None):
    several = isinstance(out_shape, (list, tuple))

    def run(*operands):
        return pl.pallas_call(
            kernel,
            out_shape=out_shape,
            in_specs=in_specs or [VMEM_SPEC] * len(operands),
            out_specs=[VMEM_SPEC] * len(out_shape) if several else VMEM_SPEC,
            scratch_shapes=list(scratch),
            compiler_params=pltpu.CompilerParams(vmem_limit_bytes=vmem * MIB),
            cost_estimate=pl.CostEstimate(
                flops=int(flops), bytes_accessed=int(size), transcendentals=int(transcendentals)
            ),
            name=name,
        )(*operands)

    return run


def in_hbm(x):
    return pltpu.with_memory_space_constraint(x, pltpu.HBM)


def rotated(x, shift):
    count = lax.axis_size("cell")
    return lax.ppermute(x, "cell", [((i + shift) % count, i) for i in range(count)])


def rounds(count):
    stride = 1
    while stride < count:
        left = count // stride
        radix = 4 if stride == 1 and left % 4 == 0 else next(r for r in range(2, left + 1) if left % r == 0)
        yield stride, radix
        stride *= radix


def swapped(x, stride, radix):
    count = lax.axis_size("study")

    def partner(i, k):
        digit = i // stride % radix
        other = digit ^ k if radix & (radix - 1) == 0 else (digit + k) % radix
        return i + (other - digit) * stride

    return [
        lax.ppermute(x, "study", [(i, partner(i, k)) for i in range(count)])
        for k in range(1, radix)
    ]


def on_device(latents, donor_ids, study_valid_length, study_penalty_weight, frequencies, phases):
    own = jnp.swapaxes(latents[0], 0, 1)
    depth, cells = own.shape
    blocks = lax.axis_size("cell")
    studies = lax.axis_size("study")
    features = frequencies.shape[1]
    split = split_features(features, blocks)
    width = split.wide
    window = blocks * cells
    mean_shape = (split.rows, width // split.rows)
    f32, bf16 = jnp.float32, jnp.bfloat16
    shape = jax.ShapeDtypeStruct
    pairs = window * width

    others = [rotated(own, k) for k in range(1, blocks)]
    donors = [donor_ids] + [rotated(donor_ids, k) for k in range(1, blocks)]

    turn_weights, freq_part, own, x_own, consts = call(
        functools.partial(setup_kernel, split),
        [
            shape((2 * PAIR, width), bf16),
            shape((depth, width), bf16),
            shape((depth, cells), bf16),
            shape((2 * PAIR, cells), bf16),
            shape((1, 128), f32),
        ],
        "setup",
        flops=20 * depth * width,
        size=4 * depth * width,
        scratch=[pltpu.VMEM((1, width), f32), pltpu.SemaphoreType.DMA((3,))],
        in_specs=[SMEM_SPEC] + [HBM_SPEC] * 3,
    )(
        study_valid_length,
        *[in_hbm(x) for x in (frequencies, phases.reshape(1, features), own)],
    )

    *halves, mean = call(
        functools.partial(cosine_kernel, split, blocks),
        [shape((width, cells), f32)] * blocks + [shape(mean_shape, f32)],
        "cosine_sums",
        flops=4 * PAIR * pairs + 12 * pairs,
        size=4 * PAIR * width,
        scratch=[pltpu.VMEM((2 * PAIR, cells), bf16)] * (blocks - 1),
    )(consts, turn_weights, x_own, *others)

    def couplings():
        return call(
            functools.partial(coupling_kernel, blocks),
            [shape((depth, cells), f32)],
            "coupling",
            flops=2 * cells * window * (3 * depth),
            transcendentals=cells * window,
            size=4 * cells * depth,
            in_specs=[SMEM_SPEC] + [VMEM_SPEC] * (1 + 2 * blocks),
        )(study_penalty_weight, consts, own, *others, *donors)

    def sine_parts(halves):
        return call(
            functools.partial(sine_kernel, split, len(halves)),
            [shape((width, cells), bf16)] * len(halves),
            "sines",
            flops=12 * pairs,
            transcendentals=pairs,
            size=6 * pairs,
        )(*halves)

    study_penalty_weight, mean = lax.optimization_barrier((study_penalty_weight, mean))
    center, own_half, done = mean, halves[0], []
    steps = [lambda: sine_parts(halves[1:]), couplings, lambda: sine_parts([own_half])]
    for stride, radix in rounds(studies):
        parts = swapped(center, stride, radix)
        made = steps[len(done)]() if len(done) < len(steps) else []
        later = [own_half] if len(done) < len(steps) - 1 else []
        center, *made = lax.optimization_barrier((sum(parts, center), *made, *later))
        if later:
            own_half = made.pop()
        if len(done) < len(steps):
            done.append(made)
    while len(done) < len(steps):
        done.append(steps[len(done)]())
    sines, bases = [*done[2], *done[0]], done[1]

    out, residual_freq = None, None
    part_shape = shape((depth, cells), f32)
    cost = dict(flops=2 * cells * width * depth, size=2 * cells * width)
    for block in range(1, blocks):
        base = bases[block : block + 1]
        if residual_freq is None:
            part, residual_freq = call(
                functools.partial(residual_kernel, split, block, window),
                [part_shape, shape((2 * depth, width), bf16)],
                "residual_part",
                **cost,
            )(consts, center, mean, freq_part, sines[block], *base)
        else:
            part = call(
                functools.partial(part_kernel, split, block, window), part_shape, "other_part", **cost
            )(consts, sines[block], residual_freq, *base)
        sent = rotated(part, blocks - block)
        out = sent if out is None else out + sent
    own_part = call(functools.partial(part_kernel, split, 0, window), part_shape, "own_part", **cost)(
        consts, sines[0], residual_freq, bases[0]
    )
    return jnp.swapaxes(own_part + out, 0, 1)[None]


def solution(mesh):
    in_specs = (P("study", "cell", None), P("study", "cell"), P("study"), P("study"), P(), P())
    out_specs = P("study", "cell", None)
    return jax.shard_map(
        on_device, mesh=mesh, in_specs=in_specs, out_specs=out_specs, check_vma=False
    )
```

```python
import functools
import math
from typing import NamedTuple

import jax
import jax.numpy as jnp
from jax import lax
from jax.experimental import pallas as pl
from jax.experimental.pallas import tpu as pltpu
from jax.sharding import PartitionSpec as P

DONOR_LABELS = 16
FEATURE_PENALTY = 16.0
BLOCK = 1024
PAIR = 128
WIDE_CORE = 1
SHIFT = 6
LANES = 128
PHASE_ROWS = 16
SUBLANES = 8
MIB = 1 << 20

COS_LEAD = -0.552051508388134
COS_TERMS = (-4.602194203577409, 9.359560663732573, -5.6907268683441155)
SIN_LEAD = 2.0 * COS_LEAD * abs(COS_LEAD)

VMEM_SPEC = pl.BlockSpec(memory_space=pltpu.VMEM)
SMEM_SPEC = pl.BlockSpec(memory_space=pltpu.SMEM)
HBM_SPEC = pl.BlockSpec(memory_space=pltpu.HBM)


def split3(x):
    hi = x.astype(jnp.bfloat16)
    rest = x - hi.astype(jnp.float32)
    mid = rest.astype(jnp.bfloat16)
    low = (rest - mid.astype(jnp.float32)).astype(jnp.bfloat16)
    return hi, mid, low


def block_start(block, cells):
    count = lax.axis_size("cell")
    return lax.rem(lax.axis_index("cell") + block, count) * cells


def valid_row(block, cells, length):
    position = lax.broadcasted_iota(jnp.int32, (1, cells), 1) + block_start(block, cells)
    return (position.astype(jnp.float32) < length).astype(jnp.float32)


class Split(NamedTuple):
    features: int
    narrow: int
    wide: int

    @property
    def scale(self):
        return math.sqrt(2.0 / self.features)

    @property
    def rows(self):
        return next(r for r in range(SUBLANES, 0, -1) if self.wide % (r * LANES) == 0)

    def start(self):
        return pl.multiple_of(lax.axis_index("cell") * self.narrow, LANES)

    def extra(self, body):
        if self.wide > self.narrow:
            pl.when(lax.axis_index("cell") == WIDE_CORE)(body)

    def over_blocks(self, body):
        def over(start, stop):
            for offset in range(start, stop, BLOCK):
                body(offset, min(BLOCK, stop - offset))

        over(0, self.narrow)
        self.extra(lambda: over(self.narrow, self.wide))


def split_features(features, blocks):
    even = features // blocks
    shift = even * SHIFT // (LANES * 32) * LANES if blocks == 2 else 0
    return Split(features, even - shift, even + shift)


def store_cells(x_ref, z, valid):
    depth, cells = z.shape
    z = (z.astype(jnp.float32) * valid).astype(jnp.bfloat16)
    for part in range(3):
        x_ref[part * depth : (part + 1) * depth, :] = z
    tail = x_ref.shape[0] - 3 * depth
    ones = jnp.where(lax.broadcasted_iota(jnp.int32, (tail, cells), 0) < 3, valid, 0.0)
    x_ref[3 * depth :, :] = ones.astype(jnp.bfloat16)


def setup_kernel(split, length_ref, freq_hbm, phase_hbm, z_hbm, w_ref, freq_ref, z_ref, x_ref, const_ref, phase_buf, sems):
    depth, width = freq_ref.shape
    start = split.start()
    copies = [
        pltpu.make_async_copy(source, target, sems.at[i])
        for i, (source, target) in enumerate(
            [
                (z_hbm, z_ref),
                (phase_hbm.at[:, pl.ds(start, width)], phase_buf),
                (freq_hbm.at[:, pl.ds(start, width)], freq_ref),
            ]
        )
    ]
    for copy in copies:
        copy.start()
    length = jnp.full((1, 1), length_ref[0], jnp.int32).astype(jnp.float32)
    const_ref[...] = jnp.broadcast_to(length, const_ref.shape)
    row = 3 * depth + PHASE_ROWS
    w_ref[row:, :] = jnp.zeros((2 * PAIR - row, width), jnp.bfloat16)
    copies[0].wait()
    store_cells(x_ref, z_ref[...], valid_row(0, z_ref.shape[1], length))
    for copy in copies[1:]:
        copy.wait()
    turn = 1.0 / (2.0 * math.pi)
    for part, rows in enumerate(split3(freq_ref[...].astype(jnp.float32) * turn)):
        w_ref[part * depth : (part + 1) * depth, :] = rows
    hi, mid, low = [p.astype(jnp.float32) for p in split3(phase_buf[...] * turn)]
    index = lax.broadcasted_iota(jnp.int32, (PHASE_ROWS, width), 0)
    rows = jnp.where(index == 0, hi, jnp.where(index == 1, mid, jnp.where(index == 2, low, 0.0)))
    w_ref[3 * depth : row, :] = rows.astype(jnp.bfloat16)


def cosine_kernel(split, blocks, const_ref, w_ref, x_own_ref, *refs):
    z_refs = refs[: blocks - 1]
    s_refs = refs[blocks - 1 : 2 * blocks - 1]
    mean_ref = refs[2 * blocks - 1]
    x_refs = [x_own_ref, *refs[2 * blocks :]]
    width, cells = s_refs[0].shape
    length = const_ref[0:1, 0:1]
    for block in range(1, blocks):
        store_cells(x_refs[block], z_refs[block - 1][...], valid_row(block, cells, length))
    scale = split.scale
    per_length = 1.0 / length
    a, b, c = COS_TERMS
    strip = mean_ref.shape[1]
    mean_ref[...] = jnp.zeros_like(mean_ref)

    def one_block(offset, size):
        here = slice(offset, offset + size)
        weights = w_ref[:, here].T
        squares = jnp.zeros((size, LANES), jnp.float32)
        for x_ref, s_ref in zip(x_refs, s_refs):
            t = jnp.dot(weights, x_ref[...], preferred_element_type=jnp.float32)
            r = t - jnp.round(t)
            u = r * r
            s = r * (((u + a) * u + b) * u + c)
            s_ref[here, :] = s
            for lane in range(0, cells, LANES):
                part = s[:, lane : lane + LANES]
                squares += part * part
        squares = jnp.sum(squares.T, axis=0, keepdims=True)
        mean = scale - (2.0 * scale * COS_LEAD * COS_LEAD) * per_length * squares
        for piece in range(0, size, LANES):
            row, column = divmod(offset + piece, strip)
            mean_ref[row : row + 1, column : column + LANES] = mean[:, piece : piece + LANES]

    split.over_blocks(one_block)


def sine_kernel(split, blocks, *refs):
    top = (1.0 + 2e-6) / (COS_LEAD * COS_LEAD)

    def one_block(offset, size):
        here = slice(offset, offset + size)
        for s_ref, out_ref in zip(refs[:blocks], refs[blocks:]):
            s = s_ref[here, :]
            rest = top - s * s
            out_ref[here, :] = (s * (rest * lax.rsqrt(rest))).astype(jnp.bfloat16)

    split.over_blocks(one_block)


def stacked(rows, cells):
    index = lax.broadcasted_iota(jnp.int32, (DONOR_LABELS, cells), 0)
    total = jnp.zeros((DONOR_LABELS, cells), jnp.float32)
    for k, row in enumerate(rows):
        if row is not None:
            total = jnp.where(index == k, row, total)
    return total.astype(jnp.bfloat16)


def coupling_kernel(blocks, weight_ref, const_ref, *refs):
    z_refs, donor_refs, out_refs = refs[:blocks], refs[blocks : 2 * blocks], refs[2 * blocks :]
    depth, cells = out_refs[0].shape
    window = blocks * cells
    f32, bf16 = jnp.float32, jnp.bfloat16
    length = const_ref[0:1, 0:1]
    inverse_n = 1.0 / length
    label = lax.broadcasted_iota(jnp.int32, (DONOR_LABELS, cells), 0)
    members = [(ref[...] == label).astype(f32) for ref in donor_refs]
    valids = [valid_row(block, cells, length) for block in range(blocks)]
    counts = sum(
        jnp.sum(member * valid, axis=1, keepdims=True)
        for member, valid in zip(members, valids)
    )
    inverse = 1.0 / jnp.maximum(counts, 1.0)
    present = jnp.sum((counts > 0.5).astype(f32), axis=0, keepdims=True)
    one = jnp.ones((1, 1), f32)
    wides = [ref[...].astype(f32) for ref in z_refs]
    norms = [
        [p.astype(f32) for p in split3(-0.5 * jnp.sum(z * z, axis=0, keepdims=True))]
        for z in wides
    ]
    shares = [
        inverse_n * jnp.sum(member * inverse, axis=0, keepdims=True) for member in members
    ]
    same_zero = jnp.zeros((3 * DONOR_LABELS, cells), bf16)
    z_zero = jnp.zeros((depth, cells), bf16)
    rights = []
    for target in range(len(out_refs)):
        rest = [p.astype(f32) for p in split3(present * inverse_n * inverse_n - shares[target])]
        member = members[target].astype(bf16)
        exponent = [z_refs[target][...], stacked([one] * 3 + norms[target], cells), same_zero]
        pair = [z_zero, stacked([None] * 6 + [one] * 3 + rest, cells), member, member, member]
        rights.append(
            jnp.concatenate(
                [jnp.concatenate(exponent, axis=0), jnp.concatenate(pair, axis=0)], axis=1
            )
        )
    totals = [jnp.zeros((PAIR, cells), f32) for _ in out_refs]
    for source in range(blocks):
        valid = valids[source]
        z = z_refs[source][...]
        minus = [p.astype(f32) for p in split3(-shares[source] * valid)]
        left = jnp.concatenate(
            [
                z,
                stacked(norms[source] + [one] * 3 + minus + [valid] * 3, cells),
                *split3(members[source] * (inverse * inverse) * valid),
            ],
            axis=0,
        ).astype(f32).T.astype(bf16)
        rows = jnp.concatenate([z, jnp.ones((PAIR - depth, cells), bf16)], axis=0)
        for target, right in enumerate(rights):
            both = jnp.dot(left, right, preferred_element_type=f32)
            coupling = both[:, cells:] * jnp.exp2(both[:, :cells] * (math.log2(math.e) / depth))
            hi = coupling.astype(bf16)
            low = (coupling - hi.astype(f32)).astype(bf16)
            totals[target] += jnp.dot(rows, hi, preferred_element_type=f32)
            totals[target] += jnp.dot(rows, low, preferred_element_type=f32)
    scale = -(2.0 * window / depth) * jnp.full((1, 1), weight_ref[0], f32)
    for target, out_ref in enumerate(out_refs):
        total = totals[target]
        gradient = wides[target] * total[depth : depth + 1] - total[:depth]
        out_ref[...] = scale * valids[target] * gradient


def residual_kernel(split, block, window, const_ref, sum_ref, mean_ref, freq_ref, s_ref, *refs):
    *base_refs, out_ref, rf_ref = refs
    rows, strip = sum_ref.shape
    depth = freq_ref.shape[0]
    center = sum_ref[...] * (1.0 / lax.axis_size("study"))
    residual = (2.0 * FEATURE_PENALTY) * (mean_ref[...] - center)
    for row in range(rows):
        here = slice(row * strip, (row + 1) * strip)
        product = freq_ref[:, here].astype(jnp.float32) * residual[row : row + 1]
        hi = product.astype(jnp.bfloat16)
        rf_ref[:depth, here] = hi
        rf_ref[depth:, here] = (product - hi.astype(jnp.float32)).astype(jnp.bfloat16)
    part_kernel(split, block, window, const_ref, s_ref, rf_ref, *base_refs, out_ref)


def part_kernel(split, block, window, const_ref, s_ref, rf_ref, *refs):
    *base_refs, out_ref = refs
    depth, cells = out_ref.shape
    length = const_ref[0:1, 0:1]
    factor = -(SIN_LEAD * window * split.scale) / length * valid_row(block, cells, length)

    def part(here):
        both = jnp.dot(rf_ref[:, here], s_ref[here, :], preferred_element_type=jnp.float32)
        return factor * (both[:depth] + both[depth:])

    out_ref[...] = sum((ref[...] for ref in base_refs), part(slice(0, split.narrow)))

    def add_extra():
        out_ref[...] += part(slice(split.narrow, split.wide))

    split.extra(add_extra)


def call(kernel, out_shape, name, flops, transcendentals=0, size=0, scratch=(), vmem=8, in_specs=None):
    several = isinstance(out_shape, (list, tuple))

    def run(*operands):
        return pl.pallas_call(
            kernel,
            out_shape=out_shape,
            in_specs=in_specs or [VMEM_SPEC] * len(operands),
            out_specs=[VMEM_SPEC] * len(out_shape) if several else VMEM_SPEC,
            scratch_shapes=list(scratch),
            compiler_params=pltpu.CompilerParams(vmem_limit_bytes=vmem * MIB),
            cost_estimate=pl.CostEstimate(
                flops=int(flops), bytes_accessed=int(size), transcendentals=int(transcendentals)
            ),
            name=name,
        )(*operands)

    return run


def in_hbm(x):
    return pltpu.with_memory_space_constraint(x, pltpu.HBM)


def rotated(x, shift):
    count = lax.axis_size("cell")
    return lax.ppermute(x, "cell", [((i + shift) % count, i) for i in range(count)])


def rounds(count):
    stride = 1
    while stride < count:
        left = count // stride
        radix = 4 if stride == 1 and left % 4 == 0 else next(r for r in range(2, left + 1) if left % r == 0)
        yield stride, radix
        stride *= radix


def swapped(x, stride, radix):
    count = lax.axis_size("study")

    def partner(i, k):
        digit = i // stride % radix
        other = digit ^ k if radix & (radix - 1) == 0 else (digit + k) % radix
        return i + (other - digit) * stride

    return [
        lax.ppermute(x, "study", [(i, partner(i, k)) for i in range(count)])
        for k in range(1, radix)
    ]


def on_device(latents, donor_ids, study_valid_length, study_penalty_weight, frequencies, phases):
    own = jnp.swapaxes(latents[0], 0, 1)
    depth, cells = own.shape
    blocks = lax.axis_size("cell")
    studies = lax.axis_size("study")
    features = frequencies.shape[1]
    split = split_features(features, blocks)
    width = split.wide
    window = blocks * cells
    mean_shape = (split.rows, width // split.rows)
    f32, bf16 = jnp.float32, jnp.bfloat16
    shape = jax.ShapeDtypeStruct
    pairs = window * width

    others = [rotated(own, k) for k in range(1, blocks)]
    donors = [donor_ids] + [rotated(donor_ids, k) for k in range(1, blocks)]

    turn_weights, freq_part, own, x_own, consts = call(
        functools.partial(setup_kernel, split),
        [
            shape((2 * PAIR, width), bf16),
            shape((depth, width), bf16),
            shape((depth, cells), bf16),
            shape((2 * PAIR, cells), bf16),
            shape((1, 128), f32),
        ],
        "setup",
        flops=20 * depth * width,
        size=4 * depth * width,
        scratch=[pltpu.VMEM((1, width), f32), pltpu.SemaphoreType.DMA((3,))],
        in_specs=[SMEM_SPEC] + [HBM_SPEC] * 3,
    )(
        study_valid_length,
        *[in_hbm(x) for x in (frequencies, phases.reshape(1, features), own)],
    )

    *halves, mean = call(
        functools.partial(cosine_kernel, split, blocks),
        [shape((width, cells), f32)] * blocks + [shape(mean_shape, f32)],
        "cosine_sums",
        flops=4 * PAIR * pairs + 12 * pairs,
        size=4 * PAIR * width,
        scratch=[pltpu.VMEM((2 * PAIR, cells), bf16)] * (blocks - 1),
    )(consts, turn_weights, x_own, *others)

    def couplings():
        return call(
            functools.partial(coupling_kernel, blocks),
            [shape((depth, cells), f32)],
            "coupling",
            flops=2 * cells * window * (3 * depth),
            transcendentals=cells * window,
            size=4 * cells * depth,
            in_specs=[SMEM_SPEC] + [VMEM_SPEC] * (1 + 2 * blocks),
        )(study_penalty_weight, consts, own, *others, *donors)

    def sine_parts(halves):
        return call(
            functools.partial(sine_kernel, split, len(halves)),
            [shape((width, cells), bf16)] * len(halves),
            "sines",
            flops=12 * pairs,
            transcendentals=pairs,
            size=6 * pairs,
        )(*halves)

    study_penalty_weight, mean = lax.optimization_barrier((study_penalty_weight, mean))
    center, own_half, done = mean, halves[0], []
    steps = [lambda: sine_parts(halves[1:]), couplings, lambda: sine_parts([own_half])]
    for stride, radix in rounds(studies):
        parts = swapped(center, stride, radix)
        made = steps[len(done)]() if len(done) < len(steps) else []
        later = [own_half] if len(done) < len(steps) - 1 else []
        center, *made = lax.optimization_barrier((sum(parts, center), *made, *later))
        if later:
            own_half = made.pop()
        if len(done) < len(steps):
            done.append(made)
    while len(done) < len(steps):
        done.append(steps[len(done)]())
    sines, bases = [*done[2], *done[0]], done[1]

    out, residual_freq = None, None
    part_shape = shape((depth, cells), f32)
    cost = dict(flops=2 * cells * width * depth, size=2 * cells * width)
    for block in range(1, blocks):
        base = bases[block : block + 1]
        if residual_freq is None:
            part, residual_freq = call(
                functools.partial(residual_kernel, split, block, window),
                [part_shape, shape((2 * depth, width), bf16)],
                "residual_part",
                **cost,
            )(consts, center, mean, freq_part, sines[block], *base)
        else:
            part = call(
                functools.partial(part_kernel, split, block, window), part_shape, "other_part", **cost
            )(consts, sines[block], residual_freq, *base)
        sent = rotated(part, blocks - block)
        out = sent if out is None else out + sent
    own_part = call(functools.partial(part_kernel, split, 0, window), part_shape, "own_part", **cost)(
        consts, sines[0], residual_freq, bases[0]
    )
    return jnp.swapaxes(own_part + out, 0, 1)[None]


def solution(mesh):
    in_specs = (P("study", "cell", None), P("study", "cell"), P("study"), P("study"), P(), P())
    out_specs = P("study", "cell", None)
    return jax.shard_map(
        on_device, mesh=mesh, in_specs=in_specs, out_specs=out_specs, check_vma=False
    )
```
